128 devices in a mesh: section: 4 (over z), ctx: 32 (over y, x, core).
Axes of the slice: x: 4, y: 4, z: 4, core: 2. Of those that a mesh axis runs over, the one named last changes fastest.
Arguments:
- text_embeds: bfloat16 [4096, 8192], P('ctx'), may hold values from -6 to 6
- patches: bfloat16 [256, 5120], P('ctx'), may hold values from -6 to 6
- vis_gain: float32 [5120], replicated, may hold values from 0.25 to 1.75
- w_merge: bfloat16 [5120, 8192], P(None, 'ctx'), may hold values from -0.078125 to 0.078125
- frame_count: int32 [32], replicated, may hold values from 0 to 2, as said below
- frame_offset: int32 [64], replicated, may hold values from 0 to 4092, as said below
- doc_ids: int32 [4096], replicated, may hold values from 0 to 7, never falling along the last dimension, each value on 1 to 2048 neighbouring positions
- norm_gain: float32 [4, 8192], P('section'), may hold values from 0.25 to 1.75
- w_key: bfloat16 [4, 8192, 512], P('section', 'ctx'), may hold values from -0.0625 to 0.0625
- w_value: bfloat16 [4, 8192, 512], P('section', 'ctx'), may hold values from -0.0625 to 0.0625
- queries: bfloat16 [4, 4096, 8192], P('section', 'ctx'), may hold values from -576 to 576
Outputs:
- layer_out: bfloat16 [4, 4096, 8192], P('section', 'ctx')
The draws below stay inside these ranges and needn't reach their ends.
Inputs may be any that keep to these rules, and one draw needn't show every extreme that they name: `frame_count`: some index of ctx uses all 2 slots. `frame_offset`: distinct multiples of 4; at most 4 of them lie among the 128 positions of one index of ctx, and some index holds exactly that many.
All inputs are finite; a program needn't handle non-finite values.
Results may differ from the reference program's by a relative error of at most 0.0071.
The reference program's roundings to bfloat16 on the way (of `patch_norm`, `merged`, `joined` and `normed`) count: a program that leaves them out, or rounds other values in their place, can miss the bound.
Values may be sent and summed in bfloat16 or wider, within the bound.
A program may use at most 320 MiB of HBM per device.

```python
import math
import jax
import jax.numpy as jnp
import numpy as np
from jax import lax

D = 8192
HD = 128
QH = 64
KVH = 4
VIS_IN = 5120
FTOK = 4
FR_DEV = 2
TOK_DEV = 128
CTXS = 32
SECTIONS = 4
LEN = 4096
NFR = 64
ALLV = 256


def draw_frame_count(key, part):
    counts = jax.random.randint(key, (CTXS,), 0, FR_DEV + 1)
    chosen = jax.random.randint(jax.random.fold_in(key, 7), (), 0, CTXS)
    return counts.at[chosen].set(FR_DEV).astype(jnp.int32)


def draw_frame_offset(key, part):
    places = TOK_DEV // FTOK
    capacity = 2 * FR_DEV
    entries = CTXS * capacity
    heavy_block = jax.random.randint(jax.random.fold_in(key, 11), (), 0, CTXS)
    entry_order = jax.random.permutation(jax.random.fold_in(key, 12), entries).astype(jnp.int32)
    entry_block = entry_order // capacity
    entry_sub = entry_order % capacity
    edge_first = (entry_sub == 0) & ((entry_block == 0) | (entry_block == CTXS - 1))
    priority = jnp.where(entry_block == heavy_block, 0, jnp.where(edge_first, 1, 2)).astype(jnp.int32)
    scores = priority * entries + jnp.arange(entries, dtype=jnp.int32)
    picked = entry_order[jnp.argsort(scores)][:NFR]
    block_keys = jax.random.split(jax.random.fold_in(key, 13), CTXS)
    place_perms = jax.vmap(lambda one_key: jax.random.permutation(one_key, places))(block_keys).astype(jnp.int32)
    block_ids = jnp.arange(CTXS, dtype=jnp.int32)
    rotation = jnp.where(block_ids == 0, 0, jnp.where(block_ids == CTXS - 1, places - 1, place_perms[:, 0])).astype(jnp.int32)
    place_table = (place_perms - place_perms[:, :1] + rotation[:, None]) % places
    picked_block = picked // capacity
    picked_sub = picked % capacity
    offsets = (picked_block * places + place_table[picked_block, picked_sub]) * FTOK
    shuffled = offsets[jax.random.permutation(jax.random.fold_in(key, 14), NFR)]
    return shuffled.astype(jnp.int32)


def draw_queries(key, part):
    full_shape = (SECTIONS, LEN, QH, HD)
    head_shape = (SECTIONS, LEN, QH, 1)
    base_key = jax.random.fold_in(key, 21)
    amp_key = jax.random.fold_in(key, 22)
    mask_key = jax.random.fold_in(key, 23)
    base_values = jnp.clip(jax.random.normal(base_key, full_shape, jnp.float32), -6.0, 6.0)
    amplitude = jnp.exp(jax.random.uniform(amp_key, head_shape, jnp.float32, math.log(24.0), math.log(80.0)))
    picked = jax.random.randint(mask_key, head_shape, 0, 32) == 0
    factor = jnp.where(picked, amplitude, 1.0)
    return (base_values * factor).reshape(SECTIONS, LEN, QH * HD).astype(jnp.bfloat16)


def shard_levels(stream_key, extent, cuts, low, top_value):
    def one(dim, parts):
        heights = jax.random.uniform(jax.random.fold_in(jax.random.fold_in(stream_key, 6), dim), (parts,), jnp.float32, low / len(cuts), top_value / len(cuts))
        return jnp.repeat(jnp.exp(heights), extent[dim] // parts).reshape((-1,) + (1,) * (len(extent) - dim - 1))

    loudness = one(*cuts[0])
    for cut in cuts[1:]:
        loudness = loudness * one(*cut)
    return loudness


def profile(count, total, bound, lean):
    loads = [(1 << 20) // math.isqrt(grade ** lean) + 1 for grade in range(2, count + 1)]
    surplus, given = total - bound - (count - 1), [1] * (count - 1)
    while surplus > 0:
        free = [i for i in range(count - 1) if given[i] < bound]
        mass, budget = sum([loads[i] for i in free]), surplus
        for i in free:
            more = min(bound - given[i], max(1, budget * loads[i] // mass), surplus)
            given[i] = given[i] + more
            surplus = surplus - more
    return np.array([bound] + given)


def ragged(rng, count, total, limit, skew):
    if count == 2:
        one = jax.random.randint(rng, (), max(1, total - limit), min(limit, total - 1) + 1)
        return jnp.stack([one, total - one])
    sizes = jnp.asarray(profile(count, total, limit, skew), jnp.int32)
    twos = (count - 1) // 2
    giver, receiver = sizes[1:1 + 2 * twos:2], sizes[2:2 + 2 * twos:2]
    slack = jnp.minimum(giver - 1, limit - receiver)
    passed = jax.random.randint(jax.random.fold_in(rng, 1), (twos,), 0, 1 << 20) % (slack + 1)
    sizes = sizes.at[1:1 + 2 * twos:2].set(giver - passed).at[2:2 + 2 * twos:2].set(receiver + passed)
    return sizes[jax.random.permutation(jax.random.fold_in(rng, 2), count)]


def bell_draw(key, dims, width, reach, shards=(), held_as=jnp.bfloat16):
    values = width * jax.random.normal(key, dims, jnp.float32)
    if shards:
        values = values * shard_levels(key, dims, shards, -0.22, 0.18)
    return jnp.clip(values, -reach, reach).astype(held_as)


def setup_inputs(seed: int = 0) -> dict:
    streams_of = jax.random.split(jax.random.key(seed), 12)
    text_embeds = bell_draw(streams_of[0], (LEN, D), 1.0, 6.0, ((0, 32),))
    patches = bell_draw(streams_of[1], (ALLV, VIS_IN), 1.0, 6.0, ((0, 32),))
    vis_gain = jnp.clip(1.0 + 0.15 * jax.random.normal(streams_of[2], (VIS_IN,), jnp.float32), 0.25, 1.75)
    w_merge = bell_draw(streams_of[3], (VIS_IN, D), VIS_IN ** -0.5, 0.078125, ((1, 32),))
    frame_count = draw_frame_count(jax.random.fold_in(streams_of[11], 71), 0)
    frame_offset = draw_frame_offset(jax.random.fold_in(streams_of[11], 71), 0)
    doc_ids = jnp.searchsorted(jnp.cumsum(ragged(streams_of[6], 8, LEN, LEN // 2, 2)), jnp.arange(LEN), side="right").astype(jnp.int32)
    norm_gain = jnp.clip(1.0 + 0.15 * jax.random.normal(streams_of[7], (SECTIONS, D), jnp.float32), 0.25, 1.75)
    w_key = bell_draw(streams_of[8], (SECTIONS, D, KVH * HD), D ** -0.5, 0.0625, ((0, 4), (1, 32)))
    w_value = bell_draw(streams_of[9], (SECTIONS, D, KVH * HD), D ** -0.5, 0.0625, ((0, 4), (1, 32)))
    queries = draw_queries(jax.random.fold_in(streams_of[11], 71), 0)
    return dict(text_embeds=text_embeds, patches=patches, vis_gain=vis_gain, w_merge=w_merge, frame_count=frame_count, frame_offset=frame_offset, doc_ids=doc_ids, norm_gain=norm_gain, w_key=w_key, w_value=w_value, queries=queries)


def rms_norm(values, gain):
    wide = values.astype(jnp.float32)
    scale = lax.rsqrt(lax.optimization_barrier(jnp.mean(wide * wide, axis=-1, keepdims=True)) + 1e-06)
    return (wide * scale * gain).astype(jnp.bfloat16)

def attend(query_rows, keys, values, doc_ids, first):
    count = query_rows.shape[0]
    groups = QH // KVH
    query = query_rows.astype(jnp.float32).reshape(count, KVH, groups, HD)
    scores = jnp.einsum('tkgd,nkd->tkgn', query, keys.astype(jnp.float32).reshape(LEN, KVH, HD)) / jnp.sqrt(jnp.float32(HD))
    qpos = first + jnp.arange(count, dtype=jnp.int32)
    kpos = jnp.arange(LEN, dtype=jnp.int32)
    qdoc = lax.dynamic_slice_in_dim(doc_ids, first, count, 0)
    allowed = (kpos[None, :] <= qpos[:, None]) & (doc_ids[None, :] == qdoc[:, None])
    scores = jnp.where(allowed[:, None, None, :], scores, -1e+30)
    top = lax.optimization_barrier(jnp.max(scores, axis=-1, keepdims=True))
    expo = jnp.exp(scores - top) * allowed[:, None, None, :]
    total = lax.optimization_barrier(jnp.sum(expo, axis=-1))
    mixed = jnp.einsum('tkgn,nkd->tkgd', expo, values.astype(jnp.float32).reshape(LEN, KVH, HD))
    return (mixed / total[..., None]).reshape(count, QH * HD)

def reference(text_embeds, patches, vis_gain, w_merge, frame_count, frame_offset, doc_ids, norm_gain, w_key, w_value, queries):
    row_index = jnp.arange(ALLV, dtype=jnp.int32)
    slot = row_index // FTOK
    owner = slot // FR_DEV
    used = slot % FR_DEV < frame_count[owner]
    dest = frame_offset[slot] + row_index % FTOK
    patch_norm = rms_norm(patches, vis_gain)
    merged = jnp.dot(patch_norm, w_merge, preferred_element_type=jnp.float32).astype(jnp.bfloat16)
    target = jnp.where(used, dest, LEN).astype(jnp.int32)
    joined = text_embeds.at[target].set(merged, mode='drop')
    hidden = joined
    block = min(128, LEN)
    outputs = []
    for section in range(SECTIONS):
        normed = rms_norm(joined, norm_gain[section])
        keys = jnp.dot(normed, w_key[section], preferred_element_type=jnp.float32).astype(jnp.bfloat16)
        values = jnp.dot(normed, w_value[section], preferred_element_type=jnp.float32).astype(jnp.bfloat16)
        blocked = queries[section].reshape(LEN // block, block, QH * HD)
        starts = jnp.arange(LEN // block, dtype=jnp.int32) * block
        mixed = lax.map(lambda pair: attend(pair[0], keys, values, doc_ids, pair[1]), (blocked, starts))
        mixed = mixed.reshape(LEN, D)
        hidden = (hidden.astype(jnp.float32) + mixed).astype(jnp.bfloat16)
        outputs.append(hidden)
    return jnp.stack(outputs)
```

```python
import math

import jax
import jax.numpy as jnp
from jax import lax
from jax.experimental import pallas as pl
from jax.experimental.pallas import tpu as pltpu
from jax.sharding import PartitionSpec as P

QH = 64
HD = 128
MESH = pl.DeviceIdType.MESH
BIG = 1e30
CHUNK_HEADS = 4
WINDOW = 9


def attend_chain_kernel(
    q_ref, kt_ref, v_ref, kx_ref, qx_ref, joined_ref, out_ref,
    mixed, hidden, stage, landed, send_sem, recv_sem,
):
    section = lax.axis_index("section")
    sections = lax.axis_size("section")
    ctx = lax.axis_index("ctx")
    chip = ctx // 2
    core = ctx % 2
    chips = kt_ref.shape[0]
    tok = q_ref.shape[0]
    span = kt_ref.shape[2]
    width = CHUNK_HEADS * HD
    chunks = q_ref.shape[1] // width
    per_kv = 16 // CHUNK_HEADS
    rate = math.log2(math.e) / math.sqrt(HD)

    before = lax.rem(section + sections - 1, sections)
    after = lax.rem(section + 1, sections)
    barrier = pltpu.get_barrier_semaphore()
    pl.semaphore_signal(barrier, inc=1, device_id={"section": before}, device_id_type=MESH)
    pl.semaphore_wait(barrier, 1)

    def hop(c):
        return pltpu.make_async_remote_copy(
            src_ref=stage.at[c], dst_ref=landed.at[c],
            send_sem=send_sem.at[c], recv_sem=recv_sem.at[c],
            device_id={"section": after}, device_id_type=MESH,
        )

    def chain(c):
        cols = pl.ds(pl.multiple_of(c * width, width), width)

        @pl.when(section == 0)
        def _():
            hidden[...] = joined_ref[:, cols]

        @pl.when(section > 0)
        def _():
            hop(c).wait_recv()
            hidden[...] = landed[c]

        fresh = (hidden[...].astype(jnp.float32) + mixed[c]).astype(jnp.bfloat16)
        out_ref[:, cols] = fresh

        @pl.when(section < sections - 1)
        def _():
            stage[c] = fresh
            hop(c).start()

    def attend(i):
        kv = i // per_kv
        kcols = pl.ds(pl.multiple_of(kv * HD, HD), HD)
        where = [lax.rem(chip + (chips - WINDOW + 1) + w, chips) for w in range(WINDOW)]
        kc = [jnp.concatenate([kt_ref[b, kcols, :], kx_ref[b]], axis=0) for b in where]
        ones = jnp.ones((span, HD), jnp.bfloat16)
        vc = [jnp.concatenate([v_ref[b, :, kcols], ones], axis=1) for b in where]
        kc = jnp.concatenate(kc, axis=1)
        vc = jnp.concatenate(vc, axis=0)
        last = (WINDOW - 1) * span
        row = lax.broadcasted_iota(jnp.int32, (tok, span), 0) + core * tok
        col = lax.broadcasted_iota(jnp.int32, (tok, span), 1)
        for h in range(CHUNK_HEADS):
            qh = q_ref[:, pl.ds(pl.multiple_of(i * width, width) + h * HD, HD)]
            qc = jnp.concatenate([qh, qx_ref[...]], axis=1)
            s = jnp.dot(qc, kc, preferred_element_type=jnp.float32)
            own = jnp.where(col <= row, s[:, last:], -BIG)
            s = jnp.concatenate([s[:, :last], own], axis=1)
            top = jnp.max(s, axis=1, keepdims=True)
            p = jnp.exp2((s - top) * rate).astype(jnp.bfloat16)
            r = jnp.dot(p, vc, preferred_element_type=jnp.float32)
            mixed[i, :, h * HD : (h + 1) * HD] = r[:, :HD] / r[:, HD:]

    def step(i, _):
        attend(i)
        c = i - section

        @pl.when(c >= 0)
        def _():
            chain(c)

        return 0

    lax.fori_loop(0, chunks, step, 0)

    def tail(i, _):
        c = i - section

        @pl.when(c < chunks)
        def _():
            chain(c)

        return 0

    lax.fori_loop(chunks, chunks + sections - 1, tail, 0)

    @pl.when(section < sections - 1)
    def _():
        def drain(c, _):
            hop(c).wait_send()
            return 0

        lax.fori_loop(0, chunks, drain, 0)


def attend_chain(query, keys_t, values, key_marks, query_marks, joined):
    tok, width = query.shape
    cols = CHUNK_HEADS * HD
    chunks = width // cols
    vmem = pl.BlockSpec(memory_space=pltpu.VMEM)
    return pl.pallas_call(
        attend_chain_kernel,
        out_shape=jax.ShapeDtypeStruct((tok, width), jnp.bfloat16),
        in_specs=[vmem] * 6,
        out_specs=vmem,
        scratch_shapes=[
            pltpu.VMEM((chunks, tok, cols), jnp.float32),
            pltpu.VMEM((tok, cols), jnp.bfloat16),
            pltpu.VMEM((chunks, tok, cols), jnp.bfloat16),
            pltpu.VMEM((chunks, tok, cols), jnp.bfloat16),
            pltpu.SemaphoreType.DMA((chunks,)),
            pltpu.SemaphoreType.DMA((chunks,)),
        ],
        compiler_params=pltpu.CompilerParams(
            collective_id=1, has_side_effects=True, vmem_limit_bytes=56 * 2**20
        ),
        cost_estimate=pl.CostEstimate(
            flops=4 * tok * width * 2304, bytes_accessed=20 * 2**20, transcendentals=tok * 64 * 2304
        ),
    )(query, keys_t, values, key_marks, query_marks, joined)


def marks(doc_ids, qdoc, chip, chips):
    lane = jnp.arange(HD, dtype=jnp.int32)
    kdoc = doc_ids.reshape(chips, 1, -1)
    later = (jnp.arange(chips, dtype=jnp.int32) > chip)[:, None, None]
    other = (kdoc != lane[None, :, None]) & (lane < 8)[None, :, None]
    key_marks = (other | (later & (lane == 8)[None, :, None])).astype(jnp.bfloat16)
    hit = (qdoc[:, None] == lane[None, :]) | (lane == 8)[None, :]
    query_marks = jnp.where(hit, -BIG, 0.0).astype(jnp.bfloat16)
    return key_marks, query_marks


def rms_norm(values, gain):
    wide = values.astype(jnp.float32)
    scale = lax.rsqrt(jnp.mean(wide * wide, axis=-1, keepdims=True) + 1e-06)
    return (wide * scale * gain).astype(jnp.bfloat16)


def shards(
    text_embeds,
    patches,
    vis_gain,
    w_merge,
    frame_count,
    frame_offset,
    doc_ids,
    norm_gain,
    w_key,
    w_value,
    queries,
):
    ctx_count = lax.axis_size("ctx")
    ctx_index = lax.axis_index("ctx")
    tok_count = text_embeds.shape[0]
    width = text_embeds.shape[1]
    slots = frame_offset.shape[0]
    slot_dev = slots // ctx_count
    column_part = jnp.dot(
        rms_norm(lax.all_gather(patches, "ctx", axis=0, tiled=True), vis_gain),
        w_merge,
        preferred_element_type=jnp.float32,
    ).astype(jnp.bfloat16)
    vision_rows = column_part.shape[0]
    frame_tok = vision_rows // slots
    row_index = jnp.arange(vision_rows, dtype=jnp.int32)
    slot = row_index // frame_tok
    owner = slot // slot_dev
    used = slot % slot_dev < frame_count[owner]
    dest = frame_offset[slot] + row_index % frame_tok
    own_pos = ctx_index * tok_count + jnp.arange(tok_count, dtype=jnp.int32)
    own_match = (dest[None, :] == own_pos[:, None]) & used[None, :]
    covered = jnp.any(own_match, axis=1)
    full_rows = lax.all_gather(column_part, "ctx", axis=1, tiled=True)
    placed = jnp.dot(
        own_match.astype(jnp.bfloat16), full_rows, preferred_element_type=jnp.float32
    ).astype(jnp.bfloat16)
    joined = jnp.where(covered[:, None], placed, text_embeds)
    kv_width = w_key.shape[2]
    qdoc = lax.dynamic_slice_in_dim(doc_ids, ctx_index * tok_count, tok_count, 0)
    normed = rms_norm(joined, norm_gain[0])
    pieces = (
        lax.all_gather(w_key[0], "ctx", axis=0, tiled=True),
        lax.all_gather(w_value[0], "ctx", axis=0, tiled=True),
    )
    key_sum = jnp.dot(normed, pieces[0], preferred_element_type=jnp.float32)
    value_sum = jnp.dot(normed, pieces[1], preferred_element_type=jnp.float32)
    keys = key_sum.astype(jnp.bfloat16)
    values = value_sum.astype(jnp.bfloat16)
    all_keys, all_values = (
        lax.all_gather(keys, "ctx", axis=0, tiled=True),
        lax.all_gather(values, "ctx", axis=0, tiled=True),
    )
    chips = ctx_count // 2
    keys_t = all_keys.reshape(chips, 2 * tok_count, kv_width).transpose(0, 2, 1)
    values_b = all_values.reshape(chips, 2 * tok_count, kv_width)
    key_marks, query_marks = marks(doc_ids, qdoc, ctx_index // 2, chips)
    result = attend_chain(queries[0], keys_t, values_b, key_marks, query_marks, joined)
    return result.reshape(1, tok_count, width)


def solution(mesh):
    return jax.shard_map(
        shards,
        mesh=mesh,
        in_specs=(
            P("ctx", None),
            P("ctx", None),
            P(),
            P(None, "ctx"),
            P(),
            P(),
            P(),
            P("section", None),
            P("section", "ctx", None),
            P("section", "ctx", None),
            P("section", "ctx", None),
        ),
        out_specs=P("section", "ctx", None),
        check_vma=False,
    )
```

```python
import math

import jax
import jax.numpy as jnp
from jax import lax
from jax.experimental import pallas as pl
from jax.experimental.pallas import tpu as pltpu
from jax.sharding import PartitionSpec as P

QH = 64
HD = 128
MESH = pl.DeviceIdType.MESH
BIG = 1e30
CHUNK_HEADS = 4
WINDOW = 9


def attend_chain_kernel(
    q_ref, kv_ref, kx_ref, qx_ref, joined_ref, out_ref,
    mixed, hidden, stage, landed, send_sem, recv_sem,
):
    section = lax.axis_index("section")
    sections = lax.axis_size("section")
    ctx = lax.axis_index("ctx")
    chip = ctx // 2
    core = ctx % 2
    chips = kv_ref.shape[1]
    tok = q_ref.shape[0]
    span = kv_ref.shape[3]
    width = CHUNK_HEADS * HD
    chunks = q_ref.shape[1] // width
    per_kv = 16 // CHUNK_HEADS
    rate = math.log2(math.e) / math.sqrt(HD)

    before = lax.rem(section + sections - 1, sections)
    after = lax.rem(section + 1, sections)
    barrier = pltpu.get_barrier_semaphore()
    pl.semaphore_signal(barrier, inc=1, device_id={"section": before}, device_id_type=MESH)
    pl.semaphore_wait(barrier, 1)

    def hop(c):
        return pltpu.make_async_remote_copy(
            src_ref=stage.at[c], dst_ref=landed.at[c],
            send_sem=send_sem.at[c], recv_sem=recv_sem.at[c],
            device_id={"section": after}, device_id_type=MESH,
        )

    def chain(c):
        cols = pl.ds(pl.multiple_of(c * width, width), width)

        @pl.when(section == 0)
        def _():
            hidden[...] = jnp.concatenate([joined_ref[2 * c], joined_ref[2 * c + 1]], axis=1)

        @pl.when(section > 0)
        def _():
            hop(c).wait_recv()
            hidden[...] = landed[c]

        fresh = (hidden[...].astype(jnp.float32) + mixed[c]).astype(jnp.bfloat16)
        out_ref[:, cols] = fresh

        @pl.when(section < sections - 1)
        def _():
            stage[c] = fresh
            hop(c).start()

    def attend(i):
        kv = i // per_kv
        kcols = pl.ds(pl.multiple_of(kv * HD, HD), HD)
        vrows = pl.ds(pl.multiple_of(kv // 2 * span, span), span)
        vcols = pl.ds(pl.multiple_of(lax.rem(kv, 2) * HD, HD), HD)
        where = [lax.rem(chip + (chips - WINDOW + 1) + w, chips) for w in range(WINDOW)]
        kc = [jnp.concatenate([kv_ref[0, b, kcols, :], kx_ref[b]], axis=0) for b in where]
        ones = jnp.ones((span, HD), jnp.bfloat16)
        vc = [jnp.concatenate([kv_ref[1, b, vrows, vcols], ones], axis=1) for b in where]
        kc = jnp.concatenate(kc, axis=1)
        vc = jnp.concatenate(vc, axis=0)
        last = (WINDOW - 1) * span
        row = lax.broadcasted_iota(jnp.int32, (tok, span), 0) + core * tok
        col = lax.broadcasted_iota(jnp.int32, (tok, span), 1)
        for h in range(CHUNK_HEADS):
            qh = q_ref[:, pl.ds(pl.multiple_of(i * width, width) + h * HD, HD)]
            qc = jnp.concatenate([qh, qx_ref[...]], axis=1)
            s = jnp.dot(qc, kc, preferred_element_type=jnp.float32)
            own = jnp.where(col <= row, s[:, last:], -BIG)
            s = jnp.concatenate([s[:, :last], own], axis=1)
            top = jnp.max(s, axis=1, keepdims=True)
            p = jnp.exp2((s - top) * rate).astype(jnp.bfloat16)
            r = jnp.dot(p, vc, preferred_element_type=jnp.float32)
            mixed[i, :, h * HD : (h + 1) * HD] = r[:, :HD] / r[:, HD:]

    def step(i, _):
        attend(i)
        c = i - section

        @pl.when(c >= 0)
        def _():
            chain(c)

        return 0

    lax.fori_loop(0, chunks, step, 0)

    def tail(i, _):
        c = i - section

        @pl.when(c < chunks)
        def _():
            chain(c)

        return 0

    lax.fori_loop(chunks, chunks + sections - 1, tail, 0)

    @pl.when(section < sections - 1)
    def _():
        def drain(c, _):
            hop(c).wait_send()
            return 0

        lax.fori_loop(0, chunks, drain, 0)


def attend_chain(query, keys_values, key_marks, query_marks, joined):
    tok, width = query.shape
    cols = CHUNK_HEADS * HD
    chunks = width // cols
    vmem = pl.BlockSpec(memory_space=pltpu.VMEM)
    return pl.pallas_call(
        attend_chain_kernel,
        out_shape=jax.ShapeDtypeStruct((tok, width), jnp.bfloat16),
        in_specs=[vmem] * 5,
        out_specs=vmem,
        scratch_shapes=[
            pltpu.VMEM((chunks, tok, cols), jnp.float32),
            pltpu.VMEM((tok, cols), jnp.bfloat16),
            pltpu.VMEM((chunks, tok, cols), jnp.bfloat16),
            pltpu.VMEM((chunks, tok, cols), jnp.bfloat16),
            pltpu.SemaphoreType.DMA((chunks,)),
            pltpu.SemaphoreType.DMA((chunks,)),
        ],
        compiler_params=pltpu.CompilerParams(
            collective_id=1, has_side_effects=True, vmem_limit_bytes=56 * 2**20
        ),
        cost_estimate=pl.CostEstimate(
            flops=4 * tok * width * 2304, bytes_accessed=20 * 2**20, transcendentals=tok * 64 * 2304
        ),
    )(query, keys_values, key_marks, query_marks, joined)


def marks(doc_ids, qdoc, chip, chips):
    lane = jnp.arange(HD, dtype=jnp.int32)
    kdoc = doc_ids.reshape(chips, 1, -1)
    later = (jnp.arange(chips, dtype=jnp.int32) > chip)[:, None, None]
    other = (kdoc != lane[None, :, None]) & (lane < 8)[None, :, None]
    key_marks = (other | (later & (lane == 8)[None, :, None])).astype(jnp.bfloat16)
    hit = (qdoc[:, None] == lane[None, :]) | (lane == 8)[None, :]
    query_marks = jnp.where(hit, -BIG, 0.0).astype(jnp.bfloat16)
    return key_marks, query_marks


def torus_gather(slot, own, place, part, send, recv):
    y, x, core = place

    def chip_at(r, q):
        dy, dx = (q, r) if part == 0 else (r, q)
        return lax.rem(y + dy + 4, 4) * 4 + lax.rem(x + dx + 4, 4)

    table = {
        "e0": (0, (0, 0), None, (1, 0), (-1, 0)),
        "e1": (1, (0, 0), None, (-1, 0), (1, 0)),
        "e2": (2, (-1, 0), 0, (1, 0), (2, 0)),
        "e3": (3, (1, 0), 1, (-1, 0), (2, 0)),
    }
    for k, r in enumerate((0, -1, 1, 2)):
        first = 4 + 4 * k
        table["f0", r] = (first, (r, 0), None, (0, 1), (r, -1))
        table["f1", r] = (first + 1, (r, 0), None, (0, -1), (r, 1))
        table["f2", r] = (first + 2, (r, -1), 0, (0, 1), (r, 2))
        table["f3", r] = (first + 3, (r, 1), 1, (0, -1), (r, 2))

    def copy(event):
        index, source, half, to, _ = table[event]
        target = slot(chip_at(*source), half)
        return pltpu.make_async_remote_copy(
            src_ref=own(half) if source == (0, 0) else target,
            dst_ref=target,
            send_sem=send.at[part, index],
            recv_sem=recv.at[part, index],
            device_id={"ctx": chip_at(*to) * 2 + core},
            device_id_type=MESH,
        )

    def start(*events):
        for event in events:
            copy(event).start()

    def wait(*events):
        for event in events:
            index, _, half, _, landed = table[event]
            target = slot(chip_at(*landed), half)
            pltpu.make_async_copy(target, target, recv.at[part, index]).wait()

    def drain():
        for event in table:
            copy(event).wait_send()

    return start, wait, drain, chip_at


def project_kernel(
    patches_ref, vis_gain_ref, w_merge_ref, target_ref, pick_ref, text_ref, gain_ref,
    w_key_ref, w_value_ref,
    kv_ref, joined_out,
    patch_buf, merged, rows_out, rows_in, text_buf, joined, normed, w_buf, acc, kv_own,
    patch_send, patch_recv, w_send, w_recv, kv_send, kv_recv, pair_send, pair_recv,
    row_sem, misc_send, misc_recv, local_sem,
):
    me = lax.axis_index("ctx")
    count = lax.axis_size("ctx")
    chip, core = me // 2, me % 2
    y, x = chip // 4, chip % 4
    place = (y, x, core)
    sibling = chip * 2 + (1 - core)
    tok = text_ref.shape[0]
    chunk = joined.shape[2]

    barrier = pltpu.get_barrier_semaphore()

    def greet(i, _):
        pl.semaphore_signal(
            barrier, inc=1, device_id={"ctx": lax.rem(me + i, count)}, device_id_type=MESH
        )
        return 0

    lax.fori_loop(1, count, greet, 0)

    wide = patches_ref[...].astype(jnp.float32)
    scale = lax.rsqrt(jnp.mean(wide * wide, axis=-1, keepdims=True) + 1e-06)
    wide = wide * scale * vis_gain_ref[...]
    half_in = wide.shape[1] // 2
    patch_buf[core, chip] = jnp.concatenate(
        [wide[:, :half_in], wide[:, half_in:]], axis=0
    ).astype(jnp.bfloat16)

    text_own = pltpu.make_async_copy(text_ref, text_buf.at[core], local_sem.at[0])
    text_own.start()

    def w_local(source):
        return pltpu.make_async_copy(source, w_buf.at[me], local_sem.at[1])

    @pl.when(core == 0)
    def _():
        w_local(w_key_ref).start()

    @pl.when(core == 1)
    def _():
        w_local(w_value_ref).start()

    pl.semaphore_wait(barrier, count - 1)

    def patch_slot(part):
        def at(c, half):
            quarter = half_in // 4
            if half is None:
                cols = pl.ds(part * 2 * quarter, 2 * quarter)
            else:
                cols = pl.ds((part * 2 + half) * quarter, quarter)
            return patch_buf.at[core, c, :, cols]

        return at

    def patch_own(part):
        return lambda half: patch_slot(part)(chip, half)

    def w_slot(part):
        def at(c, half):
            if half is None:
                return w_buf.at[c * 2 + part]
            return w_buf.at[c * 2 + part, pl.ds(half * 128, 128), :]

        return at

    def w_own(part):
        return lambda half: w_slot(part)(chip, half)

    both = range(2)
    patch = [
        torus_gather(patch_slot(p), patch_own(p), place, p, patch_send, patch_recv) for p in both
    ]
    w = [torus_gather(w_slot(p), w_own(p), place, p, w_send, w_recv) for p in both]

    for start, *_ in patch:
        start("e0", "e1", ("f0", 0), ("f1", 0))

    def to_sibling(src, dst, k):
        return pltpu.make_async_remote_copy(
            src_ref=src, dst_ref=dst, send_sem=misc_send.at[k], recv_sem=misc_recv.at[k],
            device_id={"ctx": sibling}, device_id_type=MESH,
        )

    @pl.when(core == 0)
    def _():
        to_sibling(w_value_ref, w_buf.at[me], 0).start()

    @pl.when(core == 1)
    def _():
        to_sibling(w_key_ref, w_buf.at[me], 0).start()

    text_pair = to_sibling(text_ref, text_buf.at[core], 1)
    text_pair.start()

    for start, wait, *_ in patch:
        wait("e0")
        start("e2", ("f0", -1), ("f1", -1))
        wait("e1")
        start("e3", ("f0", 1), ("f1", 1))

    w_local(w_key_ref).wait()
    pltpu.make_async_copy(w_buf.at[sibling], w_buf.at[sibling], misc_recv.at[0]).wait()
    for start, *_ in w:
        start("e0", "e1")

    for start, wait, *_ in patch:
        wait(("f0", 0))
        start(("f2", 0))
        wait(("f1", 0))
        start(("f3", 0))
    for start, wait, *_ in patch:
        wait("e2", "e3")
        start(("f0", 2), ("f1", 2))
    for start, *_ in w:
        start(("f0", 0), ("f1", 0))
    for r in (-1, 1, 2):
        for start, wait, *_ in patch:
            wait(("f0", r))
            start(("f2", r))
            wait(("f1", r))
            start(("f3", r))
    for start, wait, *_ in patch:
        for r in (0, -1, 1, 2):
            wait(("f2", r), ("f3", r))
    patch_pair = to_sibling(patch_buf.at[core], patch_buf.at[core], 2)
    patch_pair.start()

    for start, wait, *_ in w:
        wait("e0")
        start("e2", ("f0", -1), ("f1", -1))
        wait("e1")
        start("e3", ("f0", 1), ("f1", 1))

    other = patch_buf.at[1 - core]
    pltpu.make_async_copy(other, other, misc_recv.at[2]).wait()

    group = 4
    per = patch_buf.shape[1] // group

    def merge(i, _):
        rows = patch_buf[i // group, pl.ds(lax.rem(i, group) * per, per)]
        flat = rows.reshape(per * 16, half_in)
        low = jnp.dot(flat, w_merge_ref[:half_in, :], preferred_element_type=jnp.float32)
        high = jnp.dot(flat, w_merge_ref[half_in:, :], preferred_element_type=jnp.float32)
        width = low.shape[1]
        low = low.reshape(per, 16, width)[:, :8]
        high = high.reshape(per, 16, width)[:, 8:]
        merged[pl.ds(pl.multiple_of(i * per * 8, per * 8), per * 8), :] = (
            (low + high).reshape(per * 8, width).astype(jnp.bfloat16)
        )
        return 0

    lax.fori_loop(0, 2 * group, merge, 0)

    slots = rows_out.shape[1]
    which = lax.broadcasted_iota(jnp.int32, (rows_out.shape[0] * slots, merged.shape[0]), 0)
    choose = jnp.where(which == target_ref[...], 1.0, 0.0).astype(jnp.bfloat16)
    chosen = jnp.dot(choose, merged[...], preferred_element_type=jnp.float32)
    rows_out[...] = chosen.astype(jnp.bfloat16).reshape(rows_out.shape)
    rows_in[me] = rows_out[chip]

    def deliver(i, _):
        to = lax.rem(me + i, count)
        pltpu.make_async_remote_copy(
            src_ref=rows_out.at[to // 2], dst_ref=rows_in.at[me],
            send_sem=row_sem.at[0], recv_sem=row_sem.at[1],
            device_id={"ctx": to}, device_id_type=MESH,
        ).start()
        return 0

    lax.fori_loop(1, count, deliver, 0)

    for start, wait, *_ in w:
        wait(("f0", 0))
        start(("f2", 0))
        wait(("f1", 0))
        start(("f3", 0))
    for start, wait, *_ in w:
        wait("e2", "e3")
        start(("f0", 2), ("f1", 2))
    for start, wait, *_ in w:
        wait(("f0", -1))
        start(("f2", -1))
        wait(("f1", -1))
        start(("f3", -1))

    text_own.wait()
    pltpu.make_async_copy(
        text_buf.at[1 - core], text_buf.at[1 - core], misc_recv.at[1]
    ).wait()
    most = rows_in.at[pl.ds(0, count - 1)]
    pltpu.make_async_copy(most, most, row_sem.at[0]).wait()
    pltpu.make_async_copy(most, most, row_sem.at[1]).wait()

    pick = pick_ref[...]
    covered = jnp.sum(pick.astype(jnp.float32), axis=1, keepdims=True) > 0.0

    def join(i, squares):
        placed = jnp.dot(pick, rows_in[i], preferred_element_type=jnp.float32)
        cols = pl.ds(pl.multiple_of(i * chunk, chunk), chunk)
        text = text_buf[:, :, cols].reshape(2 * tok, chunk).astype(jnp.float32)
        value = jnp.where(covered, placed, text)
        joined[i] = value.astype(jnp.bfloat16)
        return squares + value * value

    squares = lax.fori_loop(
        0, count, join, jnp.zeros((2 * tok, chunk), jnp.float32), unroll=2
    )
    mean = jnp.sum(squares, axis=1, keepdims=True) / (count * chunk)
    factor = lax.rsqrt(mean + 1e-06)

    def norm(i, _):
        cols = pl.ds(pl.multiple_of(i * chunk, chunk), chunk)
        value = joined[i].astype(jnp.float32)
        normed[i] = (value * factor * gain_ref[:, cols]).astype(jnp.bfloat16)
        joined_out[i] = joined[i, pl.ds(pl.multiple_of(core * tok, tok), tok), :]
        return 0

    lax.fori_loop(0, count, norm, 0, unroll=2)

    for r in (1, 2):
        for start, wait, *_ in w:
            wait(("f0", r))
            start(("f2", r))
            wait(("f1", r))
            start(("f3", r))

    acc[...] = jnp.zeros_like(acc)

    def project(k, _):
        far = k // 4
        far = lax.rem(jnp.where(far < 2, far, 5 - far), 4)
        near = lax.rem(k, 4)
        one = 2 * (lax.rem(y + far, 4) * 4 + near)
        two = 2 * (near * 4 + lax.rem(x + far, 4)) + 1
        left = jnp.concatenate([normed[one], normed[two]], axis=1)
        right = jnp.concatenate([w_buf[one], w_buf[two]], axis=0)
        acc[...] += jnp.dot(left, right, preferred_element_type=jnp.float32)
        return 0

    lax.fori_loop(0, 12, project, 0)
    for r in (0, -1, 1, 2):
        for start, wait, *_ in w:
            wait(("f2", r), ("f3", r))
    lax.fori_loop(12, 16, project, 0)

    @pl.when(core == 0)
    def _():
        kv_own[...] = acc[...].T.astype(jnp.bfloat16)

    @pl.when(core == 1)
    def _():
        width = acc.shape[1] // 2
        kv_own[...] = jnp.concatenate([acc[:, :width], acc[:, width:]], axis=0).astype(
            jnp.bfloat16
        )

    def kv_rows(part, half):
        if half is None:
            return pl.ds(part * 256, 256)
        return pl.ds(part * 256 + half * 128, 128)

    def kv_slot(part):
        return lambda c, half: kv_ref.at[core, c, kv_rows(part, half), :]

    def kv_mine(part):
        return lambda half: kv_own.at[kv_rows(part, half), :]

    kv = [torus_gather(kv_slot(p), kv_mine(p), place, p, kv_send, kv_recv) for p in both]
    rings = {0: 0, -1: 1, 1: 2, 2: 3}

    def cross(part, r, q):
        chip_at = kv[part][3]
        index = rings[r] * 4 + rings[q]
        target = kv_slot(part)(chip_at(r, q), None)
        return pltpu.make_async_remote_copy(
            src_ref=kv_mine(part)(None) if (r, q) == (0, 0) else target,
            dst_ref=target,
            send_sem=pair_send.at[part, index],
            recv_sem=pair_recv.at[part, index],
            device_id={"ctx": sibling}, device_id_type=MESH,
        )

    own_copy = pltpu.make_async_copy(kv_own, kv_ref.at[core, chip], local_sem.at[2])
    own_copy.start()
    for start, *_ in kv:
        start("e0", "e1", ("f0", 0), ("f1", 0))
    for p in both:
        cross(p, 0, 0).start()
    for p in both:
        start, wait, *_ = kv[p]
        wait("e0")
        start("e2", ("f0", -1), ("f1", -1))
        cross(p, -1, 0).start()
        wait("e1")
        start("e3", ("f0", 1), ("f1", 1))
        cross(p, 1, 0).start()

    def second(p, r):
        start, wait, *_ = kv[p]
        wait(("f0", r))
        start(("f2", r))
        cross(p, r, -1).start()
        wait(("f1", r))
        start(("f3", r))
        cross(p, r, 1).start()

    for p in both:
        second(p, 0)
    for p in both:
        start, wait, *_ = kv[p]
        wait("e2", "e3")
        start(("f0", 2), ("f1", 2))
        cross(p, 2, 0).start()
    for r in (-1, 1, 2):
        for p in both:
            second(p, r)
    for r in (0, -1, 1, 2):
        for p in both:
            kv[p][1](("f2", r), ("f3", r))
            cross(p, r, 2).start()

    for part in both:
        for r in rings:
            for q in rings:
                landed = kv_ref.at[1 - core, kv[part][3](r, q), kv_rows(part, None), :]
                index = rings[r] * 4 + rings[q]
                pltpu.make_async_copy(landed, landed, pair_recv.at[part, index]).wait()
                cross(part, r, q).wait_send()
    own_copy.wait()
    for gather in (patch, w, kv):
        for _, _, drain, _ in gather:
            drain()
    to_sibling(w_value_ref, w_buf.at[me], 0).wait_send()
    text_pair.wait_send()
    patch_pair.wait_send()


def project(patches, vis_gain, w_merge, target, pick, text, gain, w_key, w_value):
    count = lax.axis_size("ctx")
    tok, width = text.shape
    chunk = width // count
    kv_width = w_key.shape[1]
    chips = count // 2
    vmem = pl.BlockSpec(memory_space=pltpu.VMEM)
    hbm = pl.BlockSpec(memory_space=pl.ANY)
    dma = pltpu.SemaphoreType.DMA
    return pl.pallas_call(
        project_kernel,
        out_shape=(
            jax.ShapeDtypeStruct((2, chips, kv_width, 2 * tok), jnp.bfloat16),
            jax.ShapeDtypeStruct((count, tok, chunk), jnp.bfloat16),
        ),
        in_specs=[vmem] * 5 + [hbm, vmem] + [hbm] * 2,
        out_specs=(hbm, vmem),
        scratch_shapes=[
            pltpu.VMEM((2, chips, 16, patches.shape[1] // 2), jnp.bfloat16),
            pltpu.VMEM((count * 8, chunk), jnp.bfloat16),
            pltpu.VMEM((chips, 32, chunk), jnp.bfloat16),
            pltpu.VMEM((count, 32, chunk), jnp.bfloat16),
            pltpu.VMEM((2, tok, width), jnp.bfloat16),
            pltpu.VMEM((count, 2 * tok, chunk), jnp.bfloat16),
            pltpu.VMEM((count, 2 * tok, chunk), jnp.bfloat16),
            pltpu.VMEM((count, chunk, kv_width), jnp.bfloat16),
            pltpu.VMEM((2 * tok, kv_width), jnp.float32),
            pltpu.VMEM((kv_width, 2 * tok), jnp.bfloat16),
        ]
        + [dma((2, 20))] * 6
        + [dma((2, 16))] * 2
        + [dma((2,)), dma((3,)), dma((3,)), dma((3,))],
        compiler_params=pltpu.CompilerParams(
            collective_id=2, has_side_effects=True, vmem_limit_bytes=56 * 2**20
        ),
        cost_estimate=pl.CostEstimate(
            flops=4 * 10**9, bytes_accessed=20 * 2**20, transcendentals=0
        ),
    )(patches, vis_gain, w_merge, target, pick, text, gain, w_key, w_value)


def frame_places(frame_count, frame_offset, chip, tok):
    owners = frame_count.shape[0]
    per = frame_offset.shape[0] // owners
    used = (jnp.arange(per)[None, :] < frame_count[:, None]).reshape(-1)
    block = frame_offset // tok
    slot = jnp.arange(frame_offset.shape[0])
    same = (block[None, :] == block[:, None]) & (slot[None, :] < slot[:, None])
    rank = jnp.sum(same, axis=1, dtype=jnp.int32)
    frame_tok = 4
    row = jnp.arange(frame_tok, dtype=jnp.int32)
    target = jnp.where(used, block * 16 + rank * frame_tok, -1000)[:, None] + row
    dest = frame_offset[:, None] + row
    target, dest = target.reshape(-1), dest.reshape(-1)
    lane = jnp.arange(32, dtype=jnp.int32) + chip * 32
    pos = jnp.arange(2 * tok, dtype=jnp.int32) + chip * 2 * tok
    hit = (target[None, :] == lane[:, None])[None] & (dest[None, :] == pos[:, None])[:, None]
    pick = jnp.any(hit, axis=2).astype(jnp.bfloat16)
    order = target.reshape(owners // 2, 2, -1).transpose(1, 0, 2).reshape(1, -1)
    return order, pick


def shards(
    text_embeds,
    patches,
    vis_gain,
    w_merge,
    frame_count,
    frame_offset,
    doc_ids,
    norm_gain,
    w_key,
    w_value,
    queries,
):
    ctx_index = lax.axis_index("ctx")
    tok, width = text_embeds.shape
    chip = ctx_index // 2
    order, pick = frame_places(frame_count, frame_offset, chip, tok)
    qdoc = lax.dynamic_slice_in_dim(doc_ids, ctx_index * tok, tok, 0)
    key_marks, query_marks = marks(doc_ids, qdoc, chip, lax.axis_size("ctx") // 2)
    kv, joined = project(
        patches, vis_gain[None], w_merge, order, pick, text_embeds, norm_gain, w_key[0], w_value[0]
    )
    result = attend_chain(queries[0], kv, key_marks, query_marks, joined)
    return result[None]


def solution(mesh):
    return jax.shard_map(
        shards,
        mesh=mesh,
        in_specs=(
            P("ctx", None),
            P("ctx", None),
            P(),
            P(None, "ctx"),
            P(),
            P(),
            P(),
            P("section", None),
            P("section", "ctx", None),
            P("section", "ctx", None),
            P("section", "ctx", None),
        ),
        out_specs=P("section", "ctx", None),
        check_vma=False,
    )
```

```python
import math

import jax
import jax.numpy as jnp
from jax import lax
from jax.experimental import pallas as pl
from jax.experimental.pallas import tpu as pltpu
from jax.sharding import PartitionSpec as P

QH = 64
HD = 128
MESH = pl.DeviceIdType.MESH
BIG = 1e30
CHUNK_HEADS = 4
WINDOW = 9
ROUNDS = 2


def torus_gather(slot, own, place, part, send, recv, round_=0):
    y, x, core = place

    def chip_at(r, q):
        dy, dx = (q, r) if part == 0 else (r, q)
        return lax.rem(y + dy + 4, 4) * 4 + lax.rem(x + dx + 4, 4)

    table = {
        "e0": (0, (0, 0), None, (1, 0), (-1, 0)),
        "e1": (1, (0, 0), None, (-1, 0), (1, 0)),
        "e2": (2, (-1, 0), 0, (1, 0), (2, 0)),
        "e3": (3, (1, 0), 1, (-1, 0), (2, 0)),
    }
    for k, r in enumerate((0, -1, 1, 2)):
        first = 4 + 4 * k
        table["f0", r] = (first, (r, 0), None, (0, 1), (r, -1))
        table["f1", r] = (first + 1, (r, 0), None, (0, -1), (r, 1))
        table["f2", r] = (first + 2, (r, -1), 0, (0, 1), (r, 2))
        table["f3", r] = (first + 3, (r, 1), 1, (0, -1), (r, 2))

    def copy(event):
        index, source, half, to, _ = table[event]
        target = slot(chip_at(*source), half)
        return pltpu.make_async_remote_copy(
            src_ref=own(half) if source == (0, 0) else target,
            dst_ref=target,
            send_sem=send.at[2 * round_ + part, index],
            recv_sem=recv.at[2 * round_ + part, index],
            device_id={"ctx": chip_at(*to) * 2 + core},
            device_id_type=MESH,
        )

    def start(*events):
        for event in events:
            copy(event).start()

    def wait(*events):
        for event in events:
            index, _, half, _, landed = table[event]
            target = slot(chip_at(*landed), half)
            pltpu.make_async_copy(target, target, recv.at[2 * round_ + part, index]).wait()

    def drain():
        for event in table:
            copy(event).wait_send()

    return start, wait, drain, chip_at


def one_hot(condition):
    return jnp.where(condition, 1.0, 0.0).astype(jnp.bfloat16)


def iota(shape, dim):
    return lax.broadcasted_iota(jnp.int32, shape, dim)


def frame_places(counts, offsets, chip):
    frames = offsets.shape[1]
    owners = counts.shape[1]
    rows = frames * 4
    block = offsets // 128
    within = (offsets - block * 128) // 4
    member = one_hot(iota((owners, frames), 0) == block)
    earlier = one_hot(iota((frames, frames), 0) < iota((frames, frames), 1))
    before = jnp.dot(member, earlier, preferred_element_type=jnp.float32)
    rank = jnp.sum(before * member.astype(jnp.float32), axis=0, keepdims=True)
    spread = one_hot(iota((owners, frames), 0) == iota((owners, frames), 1) // 2)
    count8 = jnp.broadcast_to(counts, (8, owners)).astype(jnp.float32).astype(jnp.bfloat16)
    count = jnp.dot(count8, spread, preferred_element_type=jnp.float32)
    used = jnp.where((iota((8, frames), 1) % 2).astype(jnp.float32) < count, 1.0, 0.0)
    line = iota((8, frames), 0)
    facts = jnp.where(
        line == 0,
        block.astype(jnp.float32),
        jnp.where(line == 1, rank, jnp.where(line == 2, within.astype(jnp.float32), used)),
    ).astype(jnp.bfloat16)
    place = iota((frames, rows), 1)
    row = place % 8
    frame = ((place % 128) // 8 * 2 + place // 128) * 2 + row // 4
    expand = one_hot(iota((frames, rows), 0) == frame)
    facts = jnp.dot(facts, expand, preferred_element_type=jnp.float32).astype(jnp.int32)
    low = iota((1, rows), 1) % 4
    target = jnp.where(facts[3:4] > 0, facts[0:1] * 16 + facts[1:2] * 4 + low, -1000)
    dest = facts[0:1] * 128 + facts[2:3] * 4 + low
    choose = one_hot(iota((owners * 16, rows), 0) == target)
    hot = one_hot(iota((32, rows), 0) + chip * 32 == target)
    spot = one_hot(iota((256, rows), 0) + chip * 256 == dest)
    pick = lax.dot_general(
        spot, hot, (((1,), (1,)), ((), ())), preferred_element_type=jnp.float32
    ).astype(jnp.bfloat16)
    return choose, pick


def window_kernel(
    patches_ref, vis_gain_ref, w_merge_hbm, count_ref, offset_ref, doc_ref, text_ref, gain_ref,
    w_key_ref, w_value_ref, query_hbm,
    out_ref,
    patch_buf, w_merge_ref, merged, rows_out, rows_in, text_buf, joined, normed, w_buf, acc, kv_own,
    kv_buf, q_ref, pick_ref, kx, qx, mixed, hidden, stage, landed,
    patch_send, patch_recv, w_send, w_recv, kv_send, kv_recv, pair_send, pair_recv,
    row_sem, misc_send, misc_recv, local_sem, hop_send, hop_recv,
):
    me = lax.axis_index("ctx")
    count = lax.axis_size("ctx")
    section = lax.axis_index("section")
    sections = lax.axis_size("section")
    chip, core = me // 2, me % 2
    y, x = chip // 4, chip % 4
    place = (y, x, core)
    sibling = chip * 2 + (1 - core)
    tok = text_ref.shape[0]
    chunk = joined.shape[2]
    chips = kv_buf.shape[1]
    span = kv_buf.shape[3]

    barrier = pltpu.get_barrier_semaphore()

    def greet(i, _):
        pl.semaphore_signal(
            barrier, inc=1, device_id={"ctx": lax.rem(me + i, count)}, device_id_type=MESH
        )
        return 0

    lax.fori_loop(1, count, greet, 0)
    before = lax.rem(section + sections - 1, sections)
    after = lax.rem(section + 1, sections)
    pl.semaphore_signal(barrier, inc=1, device_id={"section": before}, device_id_type=MESH)

    text_own = pltpu.make_async_copy(text_ref, text_buf.at[core], local_sem.at[0])
    w_merge_in = pltpu.make_async_copy(w_merge_hbm, w_merge_ref, local_sem.at[2])
    query_in = pltpu.make_async_copy(query_hbm, q_ref, local_sem.at[3])

    def w_local(source):
        return pltpu.make_async_copy(source, w_buf.at[me], local_sem.at[1])

    @pl.when(core == 0)
    def _():
        w_local(w_key_ref).start()

    @pl.when(core == 1)
    def _():
        w_local(w_value_ref).start()

    w_merge_in.start()
    text_own.start()
    query_in.start()

    wide = patches_ref[...].astype(jnp.float32)
    scale = lax.rsqrt(jnp.mean(wide * wide, axis=-1, keepdims=True) + 1e-06)
    wide = wide * scale * vis_gain_ref[...]
    half_in = wide.shape[1] // 2
    patch_buf[core, chip] = jnp.concatenate(
        [wide[:, :half_in], wide[:, half_in:]], axis=0
    ).astype(jnp.bfloat16)

    pl.semaphore_wait(barrier, count)

    def patch_slot(part):
        def at(c, half):
            quarter = half_in // 4
            if half is None:
                cols = pl.ds(part * 2 * quarter, 2 * quarter)
            else:
                cols = pl.ds((part * 2 + half) * quarter, quarter)
            return patch_buf.at[core, c, :, cols]

        return at

    def own_of(slot):
        return lambda half: slot(chip, half)

    w_cols = w_buf.shape[2] // ROUNDS

    def w_slot(part, turn):
        cols = pl.ds(turn * w_cols, w_cols)

        def at(c, half):
            rows = pl.ds(0, chunk) if half is None else pl.ds(half * (chunk // 2), chunk // 2)
            return w_buf.at[c * 2 + part, rows, cols]

        return at

    kv_part = kv_buf.shape[2] // ROUNDS // 2

    def kv_rows(part, turn, half):
        first = (turn * 2 + part) * kv_part
        if half is None:
            return pl.ds(first, kv_part)
        return pl.ds(first + half * (kv_part // 2), kv_part // 2)

    def kv_slot(part, turn):
        return lambda c, half: kv_buf.at[core, c, kv_rows(part, turn, half), :]

    def kv_mine(part, turn):
        return lambda half: kv_own.at[kv_rows(part, turn, half), :]

    both = range(2)
    patch = [
        torus_gather(patch_slot(p), own_of(patch_slot(p)), place, p, patch_send, patch_recv)
        for p in both
    ]
    w = [
        [
            torus_gather(w_slot(p, t), own_of(w_slot(p, t)), place, p, w_send, w_recv, t)
            for p in both
        ]
        for t in range(ROUNDS)
    ]
    kv = [
        [
            torus_gather(kv_slot(p, t), kv_mine(p, t), place, p, kv_send, kv_recv, t)
            for p in both
        ]
        for t in range(ROUNDS)
    ]
    rings = {0: 0, -1: 1, 1: 2, 2: 3}

    def cross(turn, part, r, q):
        chip_at = kv[turn][part][3]
        index = rings[r] * 4 + rings[q]
        target = kv_slot(part, turn)(chip_at(r, q), None)
        return pltpu.make_async_remote_copy(
            src_ref=kv_mine(part, turn)(None) if (r, q) == (0, 0) else target,
            dst_ref=target,
            send_sem=pair_send.at[2 * turn + part, index],
            recv_sem=pair_recv.at[2 * turn + part, index],
            device_id={"ctx": sibling}, device_id_type=MESH,
        )

    def ignore(p, r, q):
        pass

    def first(pair):
        for start, *_ in pair:
            start("e0", "e1")
        for start, *_ in pair:
            start(("f0", 0), ("f1", 0))

    def near(pair, also=ignore):
        for p, (start, wait, *_) in enumerate(pair):
            wait("e0")
            start("e2", ("f0", -1), ("f1", -1))
            also(p, -1, 0)
            wait("e1")
            start("e3", ("f0", 1), ("f1", 1))
            also(p, 1, 0)

    def relay(pair, r, also=ignore):
        for p, (start, wait, *_) in enumerate(pair):
            wait(("f0", r))
            start(("f2", r))
            also(p, r, -1)
            wait(("f1", r))
            start(("f3", r))
            also(p, r, 1)

    def far(pair, also=ignore):
        for p, (start, wait, *_) in enumerate(pair):
            wait("e2", "e3")
            start(("f0", 2), ("f1", 2))
            also(p, 2, 0)

    def finish(pair, also=ignore):
        for r in rings:
            for p, (_, wait, *_) in enumerate(pair):
                wait(("f2", r), ("f3", r))
                also(p, r, 2)

    def to_sibling(src, dst, k):
        return pltpu.make_async_remote_copy(
            src_ref=src, dst_ref=dst, send_sem=misc_send.at[k], recv_sem=misc_recv.at[k],
            device_id={"ctx": sibling}, device_id_type=MESH,
        )

    first(patch)

    @pl.when(core == 0)
    def _():
        to_sibling(w_value_ref, w_buf.at[me], 0).start()

    @pl.when(core == 1)
    def _():
        to_sibling(w_key_ref, w_buf.at[me], 0).start()

    text_pair = to_sibling(text_ref, text_buf.at[core], 1)
    text_pair.start()
    choose, pick = frame_places(count_ref[...], offset_ref[...], chip)
    pick_ref[...] = pick

    near(patch)
    w_local(w_key_ref).wait()
    pltpu.make_async_copy(w_buf.at[sibling], w_buf.at[sibling], misc_recv.at[0]).wait()
    for start, *_ in w[0]:
        start("e0", "e1")
    relay(patch, 0)
    far(patch)
    for start, *_ in w[0]:
        start(("f0", 0), ("f1", 0))
    for r in (-1, 1, 2):
        relay(patch, r)
    finish(patch)
    patch_pair = to_sibling(patch_buf.at[core], patch_buf.at[core], 2)
    patch_pair.start()
    near(w[0])
    other = patch_buf.at[1 - core]
    w_merge_in.wait()
    pltpu.make_async_copy(other, other, misc_recv.at[2]).wait()

    group = 4
    per = chips // group

    def merge(i, _):
        rows = patch_buf[i // group, pl.ds(lax.rem(i, group) * per, per)]
        flat = rows.reshape(per * 16, half_in)
        low = jnp.dot(flat, w_merge_ref[:half_in, :], preferred_element_type=jnp.float32)
        high = jnp.dot(flat, w_merge_ref[half_in:, :], preferred_element_type=jnp.float32)
        width = low.shape[1]
        low = low.reshape(per, 16, width)[:, :8]
        high = high.reshape(per, 16, width)[:, 8:]
        merged[pl.ds(pl.multiple_of(i * per * 8, per * 8), per * 8), :] = (
            (low + high).reshape(per * 8, width).astype(jnp.bfloat16)
        )
        return 0

    lax.fori_loop(0, 2 * group, merge, 0)
    chosen = jnp.dot(choose, merged[...], preferred_element_type=jnp.float32)
    rows_out[...] = chosen.astype(jnp.bfloat16).reshape(rows_out.shape)
    rows_in[me] = rows_out[chip]

    def deliver(i, _):
        to = lax.rem(me + i, count)
        pltpu.make_async_remote_copy(
            src_ref=rows_out.at[to // 2], dst_ref=rows_in.at[me],
            send_sem=row_sem.at[0], recv_sem=row_sem.at[1],
            device_id={"ctx": to}, device_id_type=MESH,
        ).start()
        return 0

    lax.fori_loop(1, count, deliver, 0)
    relay(w[0], 0)
    far(w[0])
    relay(w[0], -1)

    depth = iota((HD, span), 0)

    def mark(i, _):
        b = lax.rem(chip + (chips - WINDOW + 1) + i, chips)
        doc = jnp.concatenate([doc_ref[2 * b], doc_ref[2 * b + 1]], axis=1)
        late = jnp.where(b > chip, 1, 0)
        flag = jnp.where(depth < 8, jnp.where(doc != depth, 1, 0), jnp.where(depth == 8, late, 0))
        kx[i] = flag.astype(jnp.float32).astype(jnp.bfloat16)
        return 0

    lax.fori_loop(0, WINDOW, mark, 0)
    side = iota((HD, tok), 0)
    hit = (side == doc_ref[me]) | (side == 8)
    qx[...] = jnp.where(hit, -BIG, 0.0).T.astype(jnp.bfloat16)

    text_own.wait()
    pltpu.make_async_copy(
        text_buf.at[1 - core], text_buf.at[1 - core], misc_recv.at[1]
    ).wait()
    most = rows_in.at[pl.ds(0, count - 1)]
    pltpu.make_async_copy(most, most, row_sem.at[0]).wait()
    pltpu.make_async_copy(most, most, row_sem.at[1]).wait()

    picked = pick_ref[...]
    covered = jnp.sum(picked.astype(jnp.float32), axis=1, keepdims=True) > 0.0

    def join(i, squares):
        placed = jnp.dot(picked, rows_in[i], preferred_element_type=jnp.float32)
        cols = pl.ds(pl.multiple_of(i * chunk, chunk), chunk)
        text = text_buf[:, :, cols].reshape(2 * tok, chunk).astype(jnp.float32)
        value = jnp.where(covered, placed, text)
        joined[i] = value.astype(jnp.bfloat16)
        return squares + value * value

    squares = lax.fori_loop(
        0, count, join, jnp.zeros((2 * tok, chunk), jnp.float32), unroll=2
    )
    mean = jnp.sum(squares, axis=1, keepdims=True) / (count * chunk)
    factor = lax.rsqrt(mean + 1e-06)
    relay(w[0], 1)
    relay(w[0], 2)
    first(w[1])

    def norm(i, _):
        cols = pl.ds(pl.multiple_of(i * chunk, chunk), chunk)
        value = joined[i].astype(jnp.float32)
        normed[i] = (value * factor * gain_ref[:, cols]).astype(jnp.bfloat16)
        return 0

    lax.fori_loop(0, count, norm, 0, unroll=2)

    def project(turn, low, high):
        def add(k, _):
            along = k // 4
            along = lax.rem(jnp.where(along < 2, along, 5 - along), 4)
            across = lax.rem(k, 4)
            one = 2 * (lax.rem(y + along, 4) * 4 + across)
            two = 2 * (across * 4 + lax.rem(x + along, 4)) + 1
            cols = pl.ds(turn * w_cols, w_cols)
            left = jnp.concatenate([normed[one], normed[two]], axis=1)
            right = jnp.concatenate([w_buf[one, :, cols], w_buf[two, :, cols]], axis=0)
            acc[...] += jnp.dot(left, right, preferred_element_type=jnp.float32)
            return 0

        lax.fori_loop(low, high, add, 0)

    def own_block(turn):
        rows = pl.ds(turn * w_cols, w_cols)

        @pl.when(core == 0)
        def _():
            kv_own[rows, :] = acc[...].T.astype(jnp.bfloat16)

        @pl.when(core == 1)
        def _():
            kv_own[rows, :] = acc[...].astype(jnp.bfloat16)

        kv_buf[core, chip, rows, :] = kv_own[rows, :]

    def handed(turn):
        return lambda p, r, q: cross(turn, p, r, q).start()

    def spread(turn):
        first(kv[turn])
        for p in both:
            cross(turn, p, 0, 0).start()

    def arrived(turn):
        for part in both:
            for r in rings:
                for q in rings:
                    rows = kv_rows(part, turn, None)
                    block = kv_buf.at[1 - core, kv[turn][part][3](r, q), rows, :]
                    index = rings[r] * 4 + rings[q]
                    pltpu.make_async_copy(
                        block, block, pair_recv.at[2 * turn + part, index]
                    ).wait()

    acc[...] = jnp.zeros_like(acc)
    project(0, 0, 12)
    finish(w[0])
    project(0, 12, 16)
    own_block(0)
    spread(0)
    near(kv[0], handed(0))
    near(w[1])
    relay(kv[0], 0, handed(0))
    far(kv[0], handed(0))
    for r in (-1, 1, 2):
        relay(kv[0], r, handed(0))
    relay(w[1], 0)
    far(w[1])
    finish(kv[0], handed(0))
    arrived(0)
    query_in.wait()

    width = CHUNK_HEADS * HD
    chunks = q_ref.shape[1] // width
    middle = chunks // 2
    per_kv = 16 // CHUNK_HEADS
    rate = math.log2(math.e) / math.sqrt(HD)

    def hop(c):
        return pltpu.make_async_remote_copy(
            src_ref=stage.at[c], dst_ref=landed.at[c],
            send_sem=hop_send.at[c], recv_sem=hop_recv.at[c],
            device_id={"section": after}, device_id_type=MESH,
        )

    def chain(c):
        cols = pl.ds(pl.multiple_of(c * width, width), width)

        @pl.when(section == 0)
        def _():
            rows = pl.ds(pl.multiple_of(core * tok, tok), tok)
            hidden[...] = jnp.concatenate(
                [joined[2 * c, rows, :], joined[2 * c + 1, rows, :]], axis=1
            )

        @pl.when(section > 0)
        def _():
            hop(c).wait_recv()
            hidden[...] = landed[c]

        fresh = (hidden[...].astype(jnp.float32) + mixed[c]).astype(jnp.bfloat16)
        out_ref[:, cols] = fresh

        @pl.when(section < sections - 1)
        def _():
            stage[c] = fresh
            hop(c).start()

    def attend(i):
        head = i // per_kv
        kcols = pl.ds(pl.multiple_of(head * HD, HD), HD)
        vrows = pl.ds(pl.multiple_of(head // 2 * span, span), span)
        vcols = pl.ds(pl.multiple_of(lax.rem(head, 2) * HD, HD), HD)
        where = [lax.rem(chip + (chips - WINDOW + 1) + b, chips) for b in range(WINDOW)]
        kc = [
            jnp.concatenate([kv_buf[0, b, kcols, :], kx[n]], axis=0) for n, b in enumerate(where)
        ]
        ones = jnp.ones((span, HD), jnp.bfloat16)
        vc = [jnp.concatenate([kv_buf[1, b, vrows, vcols], ones], axis=1) for b in where]
        kc = jnp.concatenate(kc, axis=1)
        vc = jnp.concatenate(vc, axis=0)
        last = (WINDOW - 1) * span
        row = iota((tok, span), 0) + core * tok
        col = iota((tok, span), 1)
        for h in range(CHUNK_HEADS):
            qh = q_ref[:, pl.ds(pl.multiple_of(i * width, width) + h * HD, HD)]
            qc = jnp.concatenate([qh, qx[...]], axis=1)
            s = jnp.dot(qc, kc, preferred_element_type=jnp.float32)
            own = jnp.where(col <= row, s[:, last:], -BIG)
            s = jnp.concatenate([s[:, :last], own], axis=1)
            top = jnp.max(s, axis=1, keepdims=True)
            p = jnp.exp2((s - top) * rate).astype(jnp.bfloat16)
            r = jnp.dot(p, vc, preferred_element_type=jnp.float32)
            mixed[i, :, h * HD : (h + 1) * HD] = r[:, :HD] / r[:, HD:]

    def step(i, _):
        attend(i)
        c = i - section

        @pl.when(((i < middle) & (c >= 0)) | (c >= middle))
        def _():
            chain(c)

        @pl.when(i == 0)
        def _():
            relay(w[1], -1)

        @pl.when(i == 1)
        def _():
            relay(w[1], 1)

        @pl.when(i == 2)
        def _():
            relay(w[1], 2)

        @pl.when(i == 3)
        def _():
            acc[...] = jnp.zeros_like(acc)
            project(1, 0, 12)
            finish(w[1])
            project(1, 12, 16)
            own_block(1)
            spread(1)

        @pl.when(i == 4)
        def _():
            near(kv[1], handed(1))

        @pl.when(i == 5)
        def _():
            relay(kv[1], 0, handed(1))
            far(kv[1], handed(1))

        @pl.when(i == 6)
        def _():
            for r in (-1, 1, 2):
                relay(kv[1], r, handed(1))

        @pl.when(i == middle - 1)
        def _():
            finish(kv[1], handed(1))

            def catch_up(d, _):
                chain(middle - section + d)
                return 0

            lax.fori_loop(0, section, catch_up, 0)
            arrived(1)

        return 0

    lax.fori_loop(0, chunks, step, 0)

    def tail(d, _):
        chain(chunks - section + d)
        return 0

    lax.fori_loop(0, section, tail, 0)

    @pl.when(section < sections - 1)
    def _():
        def drain(c, _):
            hop(c).wait_send()
            return 0

        lax.fori_loop(0, chunks, drain, 0)

    for turn in range(ROUNDS):
        for part in both:
            for r in rings:
                for q in rings:
                    cross(turn, part, r, q).wait_send()
    for gather in (patch, *w, *kv):
        for _, _, drain, _ in gather:
            drain()
    to_sibling(w_value_ref, w_buf.at[me], 0).wait_send()
    text_pair.wait_send()
    patch_pair.wait_send()


def window(patches, vis_gain, w_merge, counts, offsets, docs, text, gain, w_key, w_value, query):
    count = lax.axis_size("ctx")
    tok, width = text.shape
    chunk = width // count
    kv_width = w_key.shape[1]
    chips = count // 2
    cols = CHUNK_HEADS * HD
    chunks = width // cols
    bf16, f32 = jnp.bfloat16, jnp.float32
    vmem = pl.BlockSpec(memory_space=pltpu.VMEM)
    hbm = pl.BlockSpec(memory_space=pl.ANY)
    dma = pltpu.SemaphoreType.DMA
    return pl.pallas_call(
        window_kernel,
        out_shape=jax.ShapeDtypeStruct((tok, width), bf16),
        in_specs=[vmem, vmem, hbm, vmem, vmem, vmem, hbm, vmem, hbm, hbm, hbm],
        out_specs=vmem,
        scratch_shapes=[
            pltpu.VMEM((2, chips, 16, patches.shape[1] // 2), bf16),
            pltpu.VMEM(w_merge.shape, bf16),
            pltpu.VMEM((count * 8, chunk), bf16),
            pltpu.VMEM((chips, 32, chunk), bf16),
            pltpu.VMEM((count, 32, chunk), bf16),
            pltpu.VMEM((2, tok, width), bf16),
            pltpu.VMEM((count, 2 * tok, chunk), bf16),
            pltpu.VMEM((count, 2 * tok, chunk), bf16),
            pltpu.VMEM((count, chunk, kv_width), bf16),
            pltpu.VMEM((2 * tok, kv_width // ROUNDS), f32),
            pltpu.VMEM((kv_width, 2 * tok), bf16),
            pltpu.VMEM((2, chips, kv_width, 2 * tok), bf16),
            pltpu.VMEM((tok, width), bf16),
            pltpu.VMEM((2 * tok, 32), bf16),
            pltpu.VMEM((WINDOW, HD, 2 * tok), bf16),
            pltpu.VMEM((tok, HD), bf16),
            pltpu.VMEM((chunks, tok, cols), f32),
            pltpu.VMEM((tok, cols), bf16),
            pltpu.VMEM((chunks, tok, cols), bf16),
            pltpu.VMEM((chunks, tok, cols), bf16),
        ]
        + [dma((2, 20))] * 2
        + [dma((2 * ROUNDS, 20))] * 4
        + [dma((2 * ROUNDS, 16))] * 2
        + [dma((2,)), dma((3,)), dma((3,)), dma((4,)), dma((chunks,)), dma((chunks,))],
        compiler_params=pltpu.CompilerParams(
            collective_id=1, has_side_effects=True, vmem_limit_bytes=60 * 2**20
        ),
        cost_estimate=pl.CostEstimate(
            flops=24 * 10**9, bytes_accessed=12 * 2**20, transcendentals=tok * 64 * 2304
        ),
    )(patches, vis_gain, w_merge, counts, offsets, docs, text, gain, w_key, w_value, query)


def shards(
    text_embeds,
    patches,
    vis_gain,
    w_merge,
    frame_count,
    frame_offset,
    doc_ids,
    norm_gain,
    w_key,
    w_value,
    queries,
):
    count = lax.axis_size("ctx")
    result = window(
        patches,
        vis_gain[None],
        w_merge,
        frame_count[None],
        frame_offset[None],
        doc_ids.reshape(count, 1, -1),
        text_embeds,
        norm_gain,
        w_key[0],
        w_value[0],
        queries[0],
    )
    return result[None]


def solution(mesh):
    return jax.shard_map(
        shards,
        mesh=mesh,
        in_specs=(
            P("ctx", None),
            P("ctx", None),
            P(),
            P(None, "ctx"),
            P(),
            P(),
            P(),
            P("section", None),
            P("section", "ctx", None),
            P("section", "ctx", None),
            P("section", "ctx", None),
        ),
        out_specs=P("section", "ctx", None),
        check_vma=False,
    )
```

```python
import math

import jax
import jax.numpy as jnp
from jax import lax
from jax.experimental import pallas as pl
from jax.experimental.pallas import tpu as pltpu
from jax.sharding import PartitionSpec as P

QH = 64
HD = 128
MESH = pl.DeviceIdType.MESH
BIG = 1e30
CHUNK_HEADS = 4
WINDOW = 9
ROUNDS = 2


def torus_gather(slot, own, place, part, send, recv, round_=0):
    y, x, core = place

    def chip_at(r, q):
        dy, dx = (q, r) if part == 0 else (r, q)
        return lax.rem(y + dy + 4, 4) * 4 + lax.rem(x + dx + 4, 4)

    table = {
        "e0": (0, (0, 0), None, (1, 0), (-1, 0)),
        "e1": (1, (0, 0), None, (-1, 0), (1, 0)),
        "e2": (2, (-1, 0), 0, (1, 0), (2, 0)),
        "e3": (3, (1, 0), 1, (-1, 0), (2, 0)),
    }
    for k, r in enumerate((0, -1, 1, 2)):
        first = 4 + 4 * k
        table["f0", r] = (first, (r, 0), None, (0, 1), (r, -1))
        table["f1", r] = (first + 1, (r, 0), None, (0, -1), (r, 1))
        table["f2", r] = (first + 2, (r, -1), 0, (0, 1), (r, 2))
        table["f3", r] = (first + 3, (r, 1), 1, (0, -1), (r, 2))

    def copy(event):
        index, source, half, to, _ = table[event]
        target = slot(chip_at(*source), half)
        return pltpu.make_async_remote_copy(
            src_ref=own(half) if source == (0, 0) else target,
            dst_ref=target,
            send_sem=send.at[2 * round_ + part, index],
            recv_sem=recv.at[2 * round_ + part, index],
            device_id={"ctx": chip_at(*to) * 2 + core},
            device_id_type=MESH,
        )

    def start(*events):
        for event in events:
            copy(event).start()

    def wait(*events):
        for event in events:
            index, _, half, _, landed = table[event]
            target = slot(chip_at(*landed), half)
            pltpu.make_async_copy(target, target, recv.at[2 * round_ + part, index]).wait()

    def drain():
        for event in table:
            copy(event).wait_send()

    return start, wait, drain, chip_at


def one_hot(condition):
    return jnp.where(condition, 1.0, 0.0).astype(jnp.bfloat16)


def iota(shape, dim):
    return lax.broadcasted_iota(jnp.int32, shape, dim)


def frame_places(counts, offsets, chip):
    frames = offsets.shape[1]
    owners = counts.shape[1]
    rows = frames * 4
    block = offsets // 128
    within = (offsets - block * 128) // 4
    member = one_hot(iota((owners, frames), 0) == block)
    earlier = one_hot(iota((frames, frames), 0) < iota((frames, frames), 1))
    before = jnp.dot(member, earlier, preferred_element_type=jnp.float32)
    rank = jnp.sum(before * member.astype(jnp.float32), axis=0, keepdims=True)
    spread = one_hot(iota((owners, frames), 0) == iota((owners, frames), 1) // 2)
    count8 = jnp.broadcast_to(counts, (8, owners)).astype(jnp.float32).astype(jnp.bfloat16)
    count = jnp.dot(count8, spread, preferred_element_type=jnp.float32)
    used = jnp.where((iota((8, frames), 1) % 2).astype(jnp.float32) < count, 1.0, 0.0)
    line = iota((8, frames), 0)
    facts = jnp.where(
        line == 0,
        block.astype(jnp.float32),
        jnp.where(line == 1, rank, jnp.where(line == 2, within.astype(jnp.float32), used)),
    ).astype(jnp.bfloat16)
    place = iota((frames, rows), 1)
    row = place % 8
    frame = ((place % 128) // 8 * 2 + place // 128) * 2 + row // 4
    expand = one_hot(iota((frames, rows), 0) == frame)
    facts = jnp.dot(facts, expand, preferred_element_type=jnp.float32).astype(jnp.int32)
    low = iota((1, rows), 1) % 4
    target = jnp.where(facts[3:4] > 0, facts[0:1] * 16 + facts[1:2] * 4 + low, -1000)
    dest = facts[0:1] * 128 + facts[2:3] * 4 + low
    choose = one_hot(iota((owners * 16, rows), 0) == target)
    hot = one_hot(iota((32, rows), 0) + chip * 32 == target)
    spot = one_hot(iota((256, rows), 0) + chip * 256 == dest)
    pick = lax.dot_general(
        spot, hot, (((1,), (1,)), ((), ())), preferred_element_type=jnp.float32
    ).astype(jnp.bfloat16)
    return choose, pick


def window_kernel(
    patches_ref, vis_gain_ref, w_merge_hbm, count_ref, offset_ref, doc_ref, text_ref, gain_ref,
    w_key_ref, w_value_ref, query_hbm,
    out_ref,
    patch_buf, w_merge_ref, merged, rows_out, rows_in, text_buf, joined, normed, w_buf, acc, kv_own,
    kv_buf, q_ref, pick_ref, kx, qx, mixed, hidden, stage, landed,
    patch_send, patch_recv, w_send, w_recv, kv_send, kv_recv, pair_send, pair_recv,
    row_sem, misc_send, misc_recv, local_sem, hop_send, hop_recv,
):
    me = lax.axis_index("ctx")
    count = lax.axis_size("ctx")
    section = lax.axis_index("section")
    sections = lax.axis_size("section")
    chip, core = me // 2, me % 2
    y, x = chip // 4, chip % 4
    place = (y, x, core)
    sibling = chip * 2 + (1 - core)
    tok = text_ref.shape[0]
    chunk = joined.shape[2]
    chips = kv_buf.shape[1]
    span = kv_buf.shape[3]

    barrier = pltpu.get_barrier_semaphore()

    def greet(i, _):
        peer = lax.rem(chip + i, chips) * 2 + core
        pl.semaphore_signal(barrier, inc=1, device_id={"ctx": peer}, device_id_type=MESH)
        return 0

    lax.fori_loop(1, chips, greet, 0)
    pl.semaphore_signal(barrier, inc=1, device_id={"ctx": sibling}, device_id_type=MESH)
    before = lax.rem(section + sections - 1, sections)
    after = lax.rem(section + 1, sections)
    pl.semaphore_signal(barrier, inc=1, device_id={"section": before}, device_id_type=MESH)

    text_own = pltpu.make_async_copy(text_ref, text_buf.at[core], local_sem.at[0])
    w_merge_in = pltpu.make_async_copy(w_merge_hbm, w_merge_ref, local_sem.at[2])
    query_in = pltpu.make_async_copy(query_hbm, q_ref, local_sem.at[3])

    def w_local(source):
        return pltpu.make_async_copy(source, w_buf.at[me], local_sem.at[1])

    @pl.when(core == 0)
    def _():
        w_local(w_key_ref).start()

    @pl.when(core == 1)
    def _():
        w_local(w_value_ref).start()

    w_merge_in.start()
    text_own.start()
    query_in.start()

    wide = patches_ref[...].astype(jnp.float32)
    scale = lax.rsqrt(jnp.mean(wide * wide, axis=-1, keepdims=True) + 1e-06)
    wide = wide * scale * vis_gain_ref[...]
    half_in = wide.shape[1] // 2
    patch_buf[core, chip] = jnp.concatenate(
        [wide[:, :half_in], wide[:, half_in:]], axis=0
    ).astype(jnp.bfloat16)

    pl.semaphore_wait(barrier, chips + 1)

    def patch_slot(part):
        def at(c, half):
            quarter = half_in // 4
            if half is None:
                cols = pl.ds(part * 2 * quarter, 2 * quarter)
            else:
                cols = pl.ds((part * 2 + half) * quarter, quarter)
            return patch_buf.at[core, c, :, cols]

        return at

    def own_of(slot):
        return lambda half: slot(chip, half)

    w_cols = w_buf.shape[2] // ROUNDS

    def w_slot(part, turn):
        cols = pl.ds(turn * w_cols, w_cols)

        def at(c, half):
            rows = pl.ds(0, chunk) if half is None else pl.ds(half * (chunk // 2), chunk // 2)
            return w_buf.at[c * 2 + part, rows, cols]

        return at

    kv_part = kv_buf.shape[2] // ROUNDS // 2

    def kv_rows(part, turn, half):
        first = (turn * 2 + part) * kv_part
        if half is None:
            return pl.ds(first, kv_part)
        return pl.ds(first + half * (kv_part // 2), kv_part // 2)

    def kv_slot(part, turn):
        return lambda c, half: kv_buf.at[core, c, kv_rows(part, turn, half), :]

    def kv_mine(part, turn):
        return lambda half: kv_own.at[kv_rows(part, turn, half), :]

    both = range(2)
    patch = [
        torus_gather(patch_slot(p), own_of(patch_slot(p)), place, p, patch_send, patch_recv)
        for p in both
    ]
    w = [
        [
            torus_gather(w_slot(p, t), own_of(w_slot(p, t)), place, p, w_send, w_recv, t)
            for p in both
        ]
        for t in range(ROUNDS)
    ]
    kv = [
        [
            torus_gather(kv_slot(p, t), kv_mine(p, t), place, p, kv_send, kv_recv, t)
            for p in both
        ]
        for t in range(ROUNDS)
    ]
    rings = {0: 0, -1: 1, 1: 2, 2: 3}

    def cross(turn, part, r, q):
        chip_at = kv[turn][part][3]
        index = rings[r] * 4 + rings[q]
        target = kv_slot(part, turn)(chip_at(r, q), None)
        return pltpu.make_async_remote_copy(
            src_ref=kv_mine(part, turn)(None) if (r, q) == (0, 0) else target,
            dst_ref=target,
            send_sem=pair_send.at[2 * turn + part, index],
            recv_sem=pair_recv.at[2 * turn + part, index],
            device_id={"ctx": sibling}, device_id_type=MESH,
        )

    def ignore(p, r, q):
        pass

    def first(pair):
        for start, *_ in pair:
            start("e0", "e1")
        for start, *_ in pair:
            start(("f0", 0), ("f1", 0))

    def near(pair, also=ignore):
        for p, (start, wait, *_) in enumerate(pair):
            wait("e0")
            start("e2", ("f0", -1), ("f1", -1))
            also(p, -1, 0)
            wait("e1")
            start("e3", ("f0", 1), ("f1", 1))
            also(p, 1, 0)

    def relay(pair, r, also=ignore):
        for p, (start, wait, *_) in enumerate(pair):
            wait(("f0", r))
            start(("f2", r))
            also(p, r, -1)
            wait(("f1", r))
            start(("f3", r))
            also(p, r, 1)

    def far(pair, also=ignore):
        for p, (start, wait, *_) in enumerate(pair):
            wait("e2", "e3")
            start(("f0", 2), ("f1", 2))
            also(p, 2, 0)

    def finish(pair, also=ignore):
        for r in rings:
            for p, (_, wait, *_) in enumerate(pair):
                wait(("f2", r), ("f3", r))
                also(p, r, 2)

    def to_sibling(src, dst, k):
        return pltpu.make_async_remote_copy(
            src_ref=src, dst_ref=dst, send_sem=misc_send.at[k], recv_sem=misc_recv.at[k],
            device_id={"ctx": sibling}, device_id_type=MESH,
        )

    first(patch)

    @pl.when(core == 0)
    def _():
        to_sibling(w_value_ref, w_buf.at[me], 0).start()

    @pl.when(core == 1)
    def _():
        to_sibling(w_key_ref, w_buf.at[me], 0).start()

    text_pair = to_sibling(text_ref, text_buf.at[core], 1)
    text_pair.start()
    choose, pick = frame_places(count_ref[...], offset_ref[...], chip)
    pick_ref[...] = pick

    near(patch)
    w_local(w_key_ref).wait()
    pltpu.make_async_copy(w_buf.at[sibling], w_buf.at[sibling], misc_recv.at[0]).wait()
    for start, *_ in w[0]:
        start("e0", "e1")
    relay(patch, 0)
    far(patch)
    for start, *_ in w[0]:
        start(("f0", 0), ("f1", 0))
    for r in (-1, 1, 2):
        relay(patch, r)
    finish(patch)
    patch_pair = to_sibling(patch_buf.at[core], patch_buf.at[core], 2)
    patch_pair.start()
    near(w[0])
    def merge(q):
        flat = patch_buf[q].reshape(chips * 16, half_in)
        low = jnp.dot(flat, w_merge_ref[:half_in, :], preferred_element_type=jnp.float32)
        high = jnp.dot(flat, w_merge_ref[half_in:, :], preferred_element_type=jnp.float32)
        width = low.shape[1]
        low = low.reshape(chips, 16, width)[:, :8]
        high = high.reshape(chips, 16, width)[:, 8:]
        merged[pl.ds(pl.multiple_of(q * chips * 8, chips * 8), chips * 8), :] = (
            (low + high).reshape(chips * 8, width).astype(jnp.bfloat16)
        )

    w_merge_in.wait()

    def merge_step(i, _):
        @pl.when(i == 1)
        def _():
            other = patch_buf.at[1 - core]
            pltpu.make_async_copy(other, other, misc_recv.at[2]).wait()

        merge(lax.rem(core + i, 2))
        return 0

    lax.fori_loop(0, 2, merge_step, 0)
    chosen = jnp.dot(choose, merged[...], preferred_element_type=jnp.float32)
    rows_out[...] = chosen.astype(jnp.bfloat16).reshape(rows_out.shape)
    rows_in[core, chip] = rows_out[chip]

    def deliver(i, _):
        to = lax.rem(chip + i, chips)
        pltpu.make_async_remote_copy(
            src_ref=rows_out.at[to], dst_ref=rows_in.at[core, chip],
            send_sem=row_sem.at[0], recv_sem=row_sem.at[1],
            device_id={"ctx": to * 2 + core}, device_id_type=MESH,
        ).start()
        return 0

    lax.fori_loop(1, chips, deliver, 0)
    relay(w[0], 0)
    far(w[0])
    relay(w[0], -1)

    depth = iota((HD, span), 0)

    def mark(i, _):
        b = lax.rem(chip + (chips - WINDOW + 1) + i, chips)
        doc = jnp.concatenate([doc_ref[2 * b], doc_ref[2 * b + 1]], axis=1)
        late = jnp.where(b > chip, 1, 0)
        flag = jnp.where(depth < 8, jnp.where(doc != depth, 1, 0), jnp.where(depth == 8, late, 0))
        kx[i] = flag.astype(jnp.float32).astype(jnp.bfloat16)
        return 0

    lax.fori_loop(0, WINDOW, mark, 0)
    side = iota((HD, tok), 0)
    hit = (side == doc_ref[me]) | (side == 8)
    qx[...] = jnp.where(hit, -BIG, 0.0).T.astype(jnp.bfloat16)

    most = rows_in.at[core, pl.ds(0, chips - 1)]
    pltpu.make_async_copy(most, most, row_sem.at[1]).wait()
    row_pair = to_sibling(rows_in.at[core], rows_in.at[core], 3)
    row_pair.start()
    pltpu.make_async_copy(most, most, row_sem.at[0]).wait()
    relay(w[0], 1)
    relay(w[0], 2)
    first(w[1])
    text_own.wait()
    pltpu.make_async_copy(
        text_buf.at[1 - core], text_buf.at[1 - core], misc_recv.at[1]
    ).wait()
    rest = rows_in.at[1 - core]
    pltpu.make_async_copy(rest, rest, misc_recv.at[3]).wait()

    picked = pick_ref[...]
    covered = jnp.sum(picked.astype(jnp.float32), axis=1, keepdims=True) > 0.0

    def join(i, squares):
        placed = jnp.dot(picked, rows_in[lax.rem(i, 2), i // 2], preferred_element_type=jnp.float32)
        cols = pl.ds(pl.multiple_of(i * chunk, chunk), chunk)
        text = text_buf[:, :, cols].reshape(2 * tok, chunk).astype(jnp.float32)
        value = jnp.where(covered, placed, text)
        joined[i] = value.astype(jnp.bfloat16)
        return squares + value * value

    squares = lax.fori_loop(
        0, count, join, jnp.zeros((2 * tok, chunk), jnp.float32), unroll=4
    )
    mean = jnp.sum(squares, axis=1, keepdims=True) / (count * chunk)
    factor = lax.rsqrt(mean + 1e-06)

    def norm(i, _):
        cols = pl.ds(pl.multiple_of(i * chunk, chunk), chunk)
        value = joined[i].astype(jnp.float32)
        normed[:, cols] = (value * factor * gain_ref[:, cols]).astype(jnp.bfloat16)
        return 0

    lax.fori_loop(0, count, norm, 0, unroll=4)

    def project(turn):
        cols = pl.ds(turn * w_cols, w_cols)
        deep = 8

        def add(k, _):
            lanes = pl.ds(pl.multiple_of(k * deep * chunk, deep * chunk), deep * chunk)
            right = w_buf[pl.ds(k * deep, deep), :, cols].reshape(deep * chunk, w_cols)
            acc[...] += jnp.dot(normed[:, lanes], right, preferred_element_type=jnp.float32)
            return 0

        acc[...] = jnp.zeros_like(acc)
        lax.fori_loop(0, count // deep, add, 0)

    def own_block(turn):
        rows = pl.ds(turn * w_cols, w_cols)

        @pl.when(core == 0)
        def _():
            kv_own[rows, :] = acc[...].T.astype(jnp.bfloat16)

        @pl.when(core == 1)
        def _():
            kv_own[rows, :] = acc[...].astype(jnp.bfloat16)

        kv_buf[core, chip, rows, :] = kv_own[rows, :]

    def handed(turn):
        return lambda p, r, q: cross(turn, p, r, q).start()

    def spread(turn):
        first(kv[turn])
        for p in both:
            cross(turn, p, 0, 0).start()

    def arrived(turn):
        for part in both:
            for r in rings:
                for q in rings:
                    rows = kv_rows(part, turn, None)
                    block = kv_buf.at[1 - core, kv[turn][part][3](r, q), rows, :]
                    index = rings[r] * 4 + rings[q]
                    pltpu.make_async_copy(
                        block, block, pair_recv.at[2 * turn + part, index]
                    ).wait()

    finish(w[0])
    project(0)
    own_block(0)
    spread(0)
    near(kv[0], handed(0))
    near(w[1])
    relay(kv[0], 0, handed(0))
    far(kv[0], handed(0))
    for r in (-1, 1, 2):
        relay(kv[0], r, handed(0))
    relay(w[1], 0)
    far(w[1])
    relay(w[1], -1)
    finish(kv[0], handed(0))
    arrived(0)
    query_in.wait()

    def sent(turn):
        for part in both:
            for r in rings:
                for q in rings:
                    cross(turn, part, r, q).wait_send()

    width = CHUNK_HEADS * HD
    chunks = q_ref.shape[1] // width
    middle = chunks // 2
    per_kv = 16 // CHUNK_HEADS
    rate = math.log2(math.e) / math.sqrt(HD)

    def hop(c):
        return pltpu.make_async_remote_copy(
            src_ref=stage.at[c], dst_ref=landed.at[c],
            send_sem=hop_send.at[c], recv_sem=hop_recv.at[c],
            device_id={"section": after}, device_id_type=MESH,
        )

    def chain(c):
        cols = pl.ds(pl.multiple_of(c * width, width), width)

        @pl.when(section == 0)
        def _():
            rows = pl.ds(pl.multiple_of(core * tok, tok), tok)
            hidden[...] = jnp.concatenate(
                [joined[2 * c, rows, :], joined[2 * c + 1, rows, :]], axis=1
            )

        @pl.when(section > 0)
        def _():
            hop(c).wait_recv()
            hidden[...] = landed[c]

        fresh = (hidden[...].astype(jnp.float32) + mixed[c]).astype(jnp.bfloat16)
        out_ref[:, cols] = fresh

        @pl.when(section < sections - 1)
        def _():
            stage[c] = fresh
            hop(c).start()

    def attend(i):
        head = i // per_kv
        kcols = pl.ds(pl.multiple_of(head * HD, HD), HD)
        vrows = pl.ds(pl.multiple_of(head // 2 * span, span), span)
        vcols = pl.ds(pl.multiple_of(lax.rem(head, 2) * HD, HD), HD)
        where = [lax.rem(chip + (chips - WINDOW + 1) + b, chips) for b in range(WINDOW)]
        kc = [
            jnp.concatenate([kv_buf[0, b, kcols, :], kx[n]], axis=0) for n, b in enumerate(where)
        ]
        ones = jnp.ones((span, HD), jnp.bfloat16)
        vc = [jnp.concatenate([kv_buf[1, b, vrows, vcols], ones], axis=1) for b in where]
        kc = jnp.concatenate(kc, axis=1)
        vc = jnp.concatenate(vc, axis=0)
        last = (WINDOW - 1) * span
        row = iota((tok, span), 0) + core * tok
        col = iota((tok, span), 1)
        for h in range(CHUNK_HEADS):
            qh = q_ref[:, pl.ds(pl.multiple_of(i * width, width) + h * HD, HD)]
            qc = jnp.concatenate([qh, qx[...]], axis=1)
            s = jnp.dot(qc, kc, preferred_element_type=jnp.float32)
            own = jnp.where(col <= row, s[:, last:], -BIG)
            s = jnp.concatenate([s[:, :last], own], axis=1)
            top = jnp.max(s, axis=1, keepdims=True)
            p = jnp.exp2((s - top) * rate).astype(jnp.bfloat16)
            r = jnp.dot(p, vc, preferred_element_type=jnp.float32)
            mixed[i, :, h * HD : (h + 1) * HD] = r[:, :HD] / r[:, HD:]

    def step(i, _):
        attend(i)
        c = i - section

        @pl.when(((i < middle) & (c >= 0)) | (c >= middle))
        def _():
            chain(c)

        @pl.when(i == 0)
        def _():
            relay(w[1], 1)

        @pl.when(i == 1)
        def _():
            relay(w[1], 2)

        @pl.when(i == 2)
        def _():
            finish(w[1])
            project(1)
            own_block(1)
            spread(1)

        @pl.when(i == 3)
        def _():
            near(kv[1], handed(1))

        @pl.when(i == 4)
        def _():
            relay(kv[1], 0, handed(1))
            far(kv[1], handed(1))

        @pl.when(i == 5)
        def _():
            relay(kv[1], -1, handed(1))
            relay(kv[1], 1, handed(1))

        @pl.when(i == 6)
        def _():
            relay(kv[1], 2, handed(1))

        @pl.when(i == middle - 1)
        def _():
            finish(kv[1], handed(1))

            def catch_up(d, _):
                chain(middle - section + d)
                return 0

            lax.fori_loop(0, section, catch_up, 0)
            arrived(1)

        @pl.when(i == middle)
        def _():
            for gather in (patch, w[0]):
                for _, _, drain, _ in gather:
                    drain()

        @pl.when(i == middle + 1)
        def _():
            for gather in (w[1], kv[0]):
                for _, _, drain, _ in gather:
                    drain()

        @pl.when(i == middle + 2)
        def _():
            sent(0)

        @pl.when(i == middle + 3)
        def _():
            sent(1)

        @pl.when(i == middle + 4)
        def _():
            for _, _, drain, _ in kv[1]:
                drain()

        return 0

    lax.fori_loop(0, chunks, step, 0)

    def tail(d, _):
        chain(chunks - section + d)
        return 0

    lax.fori_loop(0, section, tail, 0)

    @pl.when(section < sections - 1)
    def _():
        def drain(c, _):
            hop(c).wait_send()
            return 0

        lax.fori_loop(0, chunks, drain, 0)

    to_sibling(w_value_ref, w_buf.at[me], 0).wait_send()
    text_pair.wait_send()
    patch_pair.wait_send()
    row_pair.wait_send()


def window(patches, vis_gain, w_merge, counts, offsets, docs, text, gain, w_key, w_value, query):
    count = lax.axis_size("ctx")
    tok, width = text.shape
    chunk = width // count
    kv_width = w_key.shape[1]
    chips = count // 2
    cols = CHUNK_HEADS * HD
    chunks = width // cols
    bf16, f32 = jnp.bfloat16, jnp.float32
    vmem = pl.BlockSpec(memory_space=pltpu.VMEM)
    hbm = pl.BlockSpec(memory_space=pl.ANY)
    dma = pltpu.SemaphoreType.DMA
    return pl.pallas_call(
        window_kernel,
        out_shape=jax.ShapeDtypeStruct((tok, width), bf16),
        in_specs=[vmem, vmem, hbm, vmem, vmem, vmem, hbm, vmem, hbm, hbm, hbm],
        out_specs=vmem,
        scratch_shapes=[
            pltpu.VMEM((2, chips, 16, patches.shape[1] // 2), bf16),
            pltpu.VMEM(w_merge.shape, bf16),
            pltpu.VMEM((count * 8, chunk), bf16),
            pltpu.VMEM((chips, 32, chunk), bf16),
            pltpu.VMEM((2, chips, 32, chunk), bf16),
            pltpu.VMEM((2, tok, width), bf16),
            pltpu.VMEM((count, 2 * tok, chunk), bf16),
            pltpu.VMEM((2 * tok, width), bf16),
            pltpu.VMEM((count, chunk, kv_width), bf16),
            pltpu.VMEM((2 * tok, kv_width // ROUNDS), f32),
            pltpu.VMEM((kv_width, 2 * tok), bf16),
            pltpu.VMEM((2, chips, kv_width, 2 * tok), bf16),
            pltpu.VMEM((tok, width), bf16),
            pltpu.VMEM((2 * tok, 32), bf16),
            pltpu.VMEM((WINDOW, HD, 2 * tok), bf16),
            pltpu.VMEM((tok, HD), bf16),
            pltpu.VMEM((chunks, tok, cols), f32),
            pltpu.VMEM((tok, cols), bf16),
            pltpu.VMEM((chunks, tok, cols), bf16),
            pltpu.VMEM((chunks, tok, cols), bf16),
        ]
        + [dma((2, 20))] * 2
        + [dma((2 * ROUNDS, 20))] * 4
        + [dma((2 * ROUNDS, 16))] * 2
        + [dma((2,)), dma((4,)), dma((4,)), dma((4,)), dma((chunks,)), dma((chunks,))],
        compiler_params=pltpu.CompilerParams(
            collective_id=1, has_side_effects=True, vmem_limit_bytes=60 * 2**20
        ),
        cost_estimate=pl.CostEstimate(
            flops=24 * 10**9, bytes_accessed=12 * 2**20, transcendentals=tok * 64 * 2304
        ),
    )(patches, vis_gain, w_merge, counts, offsets, docs, text, gain, w_key, w_value, query)


def shards(
    text_embeds,
    patches,
    vis_gain,
    w_merge,
    frame_count,
    frame_offset,
    doc_ids,
    norm_gain,
    w_key,
    w_value,
    queries,
):
    count = lax.axis_size("ctx")
    result = window(
        patches,
        vis_gain[None],
        w_merge,
        frame_count[None],
        frame_offset[None],
        doc_ids.reshape(count, 1, -1),
        text_embeds,
        norm_gain,
        w_key[0],
        w_value[0],
        queries[0],
    )
    return result[None]


def solution(mesh):
    return jax.shard_map(
        shards,
        mesh=mesh,
        in_specs=(
            P("ctx", None),
            P("ctx", None),
            P(),
            P(None, "ctx"),
            P(),
            P(),
            P(),
            P("section", None),
            P("section", "ctx", None),
            P("section", "ctx", None),
            P("section", "ctx", None),
        ),
        out_specs=P("section", "ctx", None),
        check_vma=False,
    )
```

```python
import math

import jax
import jax.numpy as jnp
from jax import lax
from jax.experimental import pallas as pl
from jax.experimental.pallas import tpu as pltpu
from jax.sharding import PartitionSpec as P

QH = 64
HD = 128
MESH = pl.DeviceIdType.MESH
BIG = 1e30
CHUNK_HEADS = 4
WINDOW = 9
ROUNDS = 2


def torus_gather(slot, own, place, part, send, recv, round_=0):
    y, x, core = place

    def chip_at(r, q):
        dy, dx = (q, r) if part == 0 else (r, q)
        return lax.rem(y + dy + 4, 4) * 4 + lax.rem(x + dx + 4, 4)

    table = {
        "e0": (0, (0, 0), None, (1, 0), (-1, 0)),
        "e1": (1, (0, 0), None, (-1, 0), (1, 0)),
        "e2": (2, (-1, 0), 0, (1, 0), (2, 0)),
        "e3": (3, (1, 0), 1, (-1, 0), (2, 0)),
    }
    for k, r in enumerate((0, -1, 1, 2)):
        first = 4 + 4 * k
        table["f0", r] = (first, (r, 0), None, (0, 1), (r, -1))
        table["f1", r] = (first + 1, (r, 0), None, (0, -1), (r, 1))
        table["f2", r] = (first + 2, (r, -1), 0, (0, 1), (r, 2))
        table["f3", r] = (first + 3, (r, 1), 1, (0, -1), (r, 2))

    def copy(event):
        index, source, half, to, _ = table[event]
        target = slot(chip_at(*source), half)
        return pltpu.make_async_remote_copy(
            src_ref=own(half) if source == (0, 0) else target,
            dst_ref=target,
            send_sem=send.at[2 * round_ + part, index],
            recv_sem=recv.at[2 * round_ + part, index],
            device_id={"ctx": chip_at(*to) * 2 + core},
            device_id_type=MESH,
        )

    def start(*events):
        for event in events:
            copy(event).start()

    def wait(*events):
        for event in events:
            index, _, half, _, landed = table[event]
            target = slot(chip_at(*landed), half)
            pltpu.make_async_copy(target, target, recv.at[2 * round_ + part, index]).wait()

    def drain():
        for event in table:
            copy(event).wait_send()

    return start, wait, drain, chip_at


def one_hot(condition):
    return jnp.where(condition, 1.0, 0.0).astype(jnp.bfloat16)


def iota(shape, dim):
    return lax.broadcasted_iota(jnp.int32, shape, dim)


def frame_places(counts, offsets, chip):
    frames = offsets.shape[1]
    owners = counts.shape[1]
    rows = frames * 4
    block = offsets // 128
    within = (offsets - block * 128) // 4
    member = one_hot(iota((owners, frames), 0) == block)
    earlier = one_hot(iota((frames, frames), 0) < iota((frames, frames), 1))
    before = jnp.dot(member, earlier, preferred_element_type=jnp.float32)
    rank = jnp.sum(before * member.astype(jnp.float32), axis=0, keepdims=True)
    spread = one_hot(iota((owners, frames), 0) == iota((owners, frames), 1) // 2)
    count8 = jnp.broadcast_to(counts, (8, owners)).astype(jnp.float32).astype(jnp.bfloat16)
    count = jnp.dot(count8, spread, preferred_element_type=jnp.float32)
    used = jnp.where((iota((8, frames), 1) % 2).astype(jnp.float32) < count, 1.0, 0.0)
    line = iota((8, frames), 0)
    facts = jnp.where(
        line == 0,
        block.astype(jnp.float32),
        jnp.where(line == 1, rank, jnp.where(line == 2, within.astype(jnp.float32), used)),
    ).astype(jnp.bfloat16)
    place = iota((frames, rows), 1)
    row = place % 8
    frame = ((place % 128) // 8 * 2 + place // 128) * 2 + row // 4
    expand = one_hot(iota((frames, rows), 0) == frame)
    facts = jnp.dot(facts, expand, preferred_element_type=jnp.float32).astype(jnp.int32)
    low = iota((1, rows), 1) % 4
    target = jnp.where(facts[3:4] > 0, facts[0:1] * 16 + facts[1:2] * 4 + low, -1000)
    dest = facts[0:1] * 128 + facts[2:3] * 4 + low
    choose = one_hot(iota((owners * 16, rows), 0) == target)
    hot = one_hot(iota((32, rows), 0) + chip * 32 == target)
    spot = one_hot(iota((256, rows), 0) + chip * 256 == dest)
    pick = lax.dot_general(
        spot, hot, (((1,), (1,)), ((), ())), preferred_element_type=jnp.float32
    ).astype(jnp.bfloat16)
    return choose, pick


def window_kernel(
    patches_ref, vis_gain_ref, w_merge_hbm, count_ref, offset_ref, doc_ref, text_ref, gain_ref,
    w_key_ref, w_value_ref, query_hbm,
    out_ref,
    patch_buf, w_merge_ref, merged, rows_out, rows_in, text_buf, joined, normed, w_buf, acc, kv_own,
    kv_buf, q_ref, pick_ref, kx, qx, mixed, hidden, stage, landed,
    patch_send, patch_recv, w_send, w_recv, kv_send, kv_recv, pair_send, pair_recv,
    row_sem, misc_send, misc_recv, local_sem, hop_send, hop_recv,
):
    me = lax.axis_index("ctx")
    count = lax.axis_size("ctx")
    section = lax.axis_index("section")
    sections = lax.axis_size("section")
    chip, core = me // 2, me % 2
    y, x = chip // 4, chip % 4
    place = (y, x, core)
    sibling = chip * 2 + (1 - core)
    tok = text_ref.shape[0]
    chunk = joined.shape[2]
    chips = kv_buf.shape[1]
    span = kv_buf.shape[3]

    barrier = pltpu.get_barrier_semaphore()

    def greet(i, _):
        peer = lax.rem(chip + i, chips) * 2 + core
        pl.semaphore_signal(barrier, inc=1, device_id={"ctx": peer}, device_id_type=MESH)
        return 0

    lax.fori_loop(1, chips, greet, 0)
    pl.semaphore_signal(barrier, inc=1, device_id={"ctx": sibling}, device_id_type=MESH)
    before = lax.rem(section + sections - 1, sections)
    after = lax.rem(section + 1, sections)
    pl.semaphore_signal(barrier, inc=1, device_id={"section": before}, device_id_type=MESH)

    text_own = pltpu.make_async_copy(text_ref, text_buf.at[core], local_sem.at[0])
    w_merge_in = pltpu.make_async_copy(w_merge_hbm, w_merge_ref, local_sem.at[2])
    query_in = pltpu.make_async_copy(query_hbm, q_ref, local_sem.at[3])

    def w_local(source):
        return pltpu.make_async_copy(source, w_buf.at[me], local_sem.at[1])

    @pl.when(core == 0)
    def _():
        w_local(w_key_ref).start()

    @pl.when(core == 1)
    def _():
        w_local(w_value_ref).start()

    w_merge_in.start()
    text_own.start()
    query_in.start()

    wide = patches_ref[...].astype(jnp.float32)
    scale = lax.rsqrt(jnp.mean(wide * wide, axis=-1, keepdims=True) + 1e-06)
    wide = wide * scale * vis_gain_ref[...]
    half_in = wide.shape[1] // 2
    patch_buf[core, chip] = jnp.concatenate(
        [wide[:, :half_in], wide[:, half_in:]], axis=0
    ).astype(jnp.bfloat16)

    pl.semaphore_wait(barrier, chips + 1)

    def patch_slot(part):
        def at(c, half):
            quarter = half_in // 4
            if half is None:
                cols = pl.ds(part * 2 * quarter, 2 * quarter)
            else:
                cols = pl.ds((part * 2 + half) * quarter, quarter)
            return patch_buf.at[core, c, :, cols]

        return at

    def own_of(slot):
        return lambda half: slot(chip, half)

    w_cols = w_buf.shape[2] // ROUNDS

    def w_slot(part, turn):
        cols = pl.ds(turn * w_cols, w_cols)

        def at(c, half):
            rows = pl.ds(0, chunk) if half is None else pl.ds(half * (chunk // 2), chunk // 2)
            return w_buf.at[c * 2 + part, rows, cols]

        return at

    kv_part = kv_buf.shape[2] // ROUNDS // 2

    def kv_rows(part, turn, half):
        first = (turn * 2 + part) * kv_part
        if half is None:
            return pl.ds(first, kv_part)
        return pl.ds(first + half * (kv_part // 2), kv_part // 2)

    def kv_slot(part, turn):
        return lambda c, half: kv_buf.at[core, c, kv_rows(part, turn, half), :]

    def kv_mine(part, turn):
        return lambda half: kv_own.at[kv_rows(part, turn, half), :]

    both = range(2)
    patch = [
        torus_gather(patch_slot(p), own_of(patch_slot(p)), place, p, patch_send, patch_recv)
        for p in both
    ]
    w = [
        [
            torus_gather(w_slot(p, t), own_of(w_slot(p, t)), place, p, w_send, w_recv, t)
            for p in both
        ]
        for t in range(ROUNDS)
    ]
    kv = [
        [
            torus_gather(kv_slot(p, t), kv_mine(p, t), place, p, kv_send, kv_recv, t)
            for p in both
        ]
        for t in range(ROUNDS)
    ]
    rings = {0: 0, -1: 1, 1: 2, 2: 3}

    def cross(turn, part, r, q):
        chip_at = kv[turn][part][3]
        index = rings[r] * 4 + rings[q]
        target = kv_slot(part, turn)(chip_at(r, q), None)
        return pltpu.make_async_remote_copy(
            src_ref=kv_mine(part, turn)(None) if (r, q) == (0, 0) else target,
            dst_ref=target,
            send_sem=pair_send.at[2 * turn + part, index],
            recv_sem=pair_recv.at[2 * turn + part, index],
            device_id={"ctx": sibling}, device_id_type=MESH,
        )

    def ignore(p, r, q):
        pass

    def first(pair):
        for start, *_ in pair:
            start("e0", "e1")
        for start, *_ in pair:
            start(("f0", 0), ("f1", 0))

    def near(pair, also=ignore):
        for p, (start, wait, *_) in enumerate(pair):
            wait("e0")
            start("e2", ("f0", -1), ("f1", -1))
            also(p, -1, 0)
            wait("e1")
            start("e3", ("f0", 1), ("f1", 1))
            also(p, 1, 0)

    def relay(pair, r, also=ignore):
        for p, (start, wait, *_) in enumerate(pair):
            wait(("f0", r))
            start(("f2", r))
            also(p, r, -1)
            wait(("f1", r))
            start(("f3", r))
            also(p, r, 1)

    def far(pair, also=ignore):
        for p, (start, wait, *_) in enumerate(pair):
            wait("e2", "e3")
            start(("f0", 2), ("f1", 2))
            also(p, 2, 0)

    def finish(pair, also=ignore):
        for r in rings:
            for p, (_, wait, *_) in enumerate(pair):
                wait(("f2", r), ("f3", r))
                also(p, r, 2)

    def to_sibling(src, dst, k):
        return pltpu.make_async_remote_copy(
            src_ref=src, dst_ref=dst, send_sem=misc_send.at[k], recv_sem=misc_recv.at[k],
            device_id={"ctx": sibling}, device_id_type=MESH,
        )

    first(patch)

    @pl.when(core == 0)
    def _():
        to_sibling(w_value_ref, w_buf.at[me], 0).start()

    @pl.when(core == 1)
    def _():
        to_sibling(w_key_ref, w_buf.at[me], 0).start()

    text_pair = to_sibling(text_ref, text_buf.at[core], 1)
    text_pair.start()
    choose, pick = frame_places(count_ref[...], offset_ref[...], chip)
    pick_ref[...] = pick

    near(patch)
    w_local(w_key_ref).wait()
    pltpu.make_async_copy(w_buf.at[sibling], w_buf.at[sibling], misc_recv.at[0]).wait()
    for start, *_ in w[0]:
        start("e0", "e1")
    relay(patch, 0)
    far(patch)
    for start, *_ in w[0]:
        start(("f0", 0), ("f1", 0))
    for r in (-1, 1, 2):
        relay(patch, r)
    finish(patch)
    patch_pair = to_sibling(patch_buf.at[core], patch_buf.at[core], 2)
    patch_pair.start()
    near(w[0])
    def merge(q):
        flat = patch_buf[q].reshape(chips * 16, half_in)
        low = jnp.dot(flat, w_merge_ref[:half_in, :], preferred_element_type=jnp.float32)
        high = jnp.dot(flat, w_merge_ref[half_in:, :], preferred_element_type=jnp.float32)
        width = low.shape[1]
        low = low.reshape(chips, 16, width)[:, :8]
        high = high.reshape(chips, 16, width)[:, 8:]
        merged[pl.ds(pl.multiple_of(q * chips * 8, chips * 8), chips * 8), :] = (
            (low + high).reshape(chips * 8, width).astype(jnp.bfloat16)
        )

    w_merge_in.wait()

    def merge_step(i, _):
        @pl.when(i == 1)
        def _():
            other = patch_buf.at[1 - core]
            pltpu.make_async_copy(other, other, misc_recv.at[2]).wait()

        merge(lax.rem(core + i, 2))
        return 0

    lax.fori_loop(0, 2, merge_step, 0)
    chosen = jnp.dot(choose, merged[...], preferred_element_type=jnp.float32)
    rows_out[...] = chosen.astype(jnp.bfloat16).reshape(rows_out.shape)
    rows_in[core, chip] = rows_out[chip]

    def deliver(i, _):
        to = lax.rem(chip + i, chips)
        pltpu.make_async_remote_copy(
            src_ref=rows_out.at[to], dst_ref=rows_in.at[core, chip],
            send_sem=row_sem.at[0], recv_sem=row_sem.at[1],
            device_id={"ctx": to * 2 + core}, device_id_type=MESH,
        ).start()
        return 0

    lax.fori_loop(1, chips, deliver, 0)
    relay(w[0], 0)
    far(w[0])
    relay(w[0], -1)

    depth = iota((HD, span), 0)

    def mark(i, _):
        b = lax.rem(chip + (chips - WINDOW + 1) + i, chips)
        doc = jnp.concatenate([doc_ref[2 * b], doc_ref[2 * b + 1]], axis=1)
        late = jnp.where(b > chip, 1, 0)
        flag = jnp.where(depth < 8, jnp.where(doc != depth, 1, 0), jnp.where(depth == 8, late, 0))
        kx[i] = flag.astype(jnp.float32).astype(jnp.bfloat16)
        return 0

    lax.fori_loop(0, WINDOW, mark, 0)
    side = iota((HD, tok), 0)
    hit = (side == doc_ref[me]) | (side == 8)
    qx[...] = jnp.where(hit, -BIG, 0.0).T.astype(jnp.bfloat16)

    most = rows_in.at[core, pl.ds(0, chips - 1)]
    pltpu.make_async_copy(most, most, row_sem.at[1]).wait()
    row_pair = to_sibling(rows_in.at[core], rows_in.at[core], 3)
    row_pair.start()
    pltpu.make_async_copy(most, most, row_sem.at[0]).wait()
    relay(w[0], 1)
    relay(w[0], 2)
    text_own.wait()
    pltpu.make_async_copy(
        text_buf.at[1 - core], text_buf.at[1 - core], misc_recv.at[1]
    ).wait()
    rest = rows_in.at[1 - core]
    pltpu.make_async_copy(rest, rest, misc_recv.at[3]).wait()

    picked = pick_ref[...]
    covered = jnp.sum(picked.astype(jnp.float32), axis=1, keepdims=True) > 0.0

    def join(i, squares):
        placed = jnp.dot(picked, rows_in[lax.rem(i, 2), i // 2], preferred_element_type=jnp.float32)
        cols = pl.ds(pl.multiple_of(i * chunk, chunk), chunk)
        text = text_buf[:, :, cols].reshape(2 * tok, chunk).astype(jnp.float32)
        value = jnp.where(covered, placed, text)
        joined[i] = value.astype(jnp.bfloat16)
        return squares + value * value

    squares = lax.fori_loop(
        0, count, join, jnp.zeros((2 * tok, chunk), jnp.float32), unroll=4
    )
    mean = jnp.sum(squares, axis=1, keepdims=True) / (count * chunk)
    factor = lax.rsqrt(mean + 1e-06)

    def norm(i, _):
        cols = pl.ds(pl.multiple_of(i * chunk, chunk), chunk)
        value = joined[i].astype(jnp.float32)
        normed[:, cols] = (value * factor * gain_ref[:, cols]).astype(jnp.bfloat16)
        return 0

    lax.fori_loop(0, count, norm, 0, unroll=4)

    def project(turn):
        cols = pl.ds(turn * w_cols, w_cols)
        deep = 8

        def add(k, _):
            lanes = pl.ds(pl.multiple_of(k * deep * chunk, deep * chunk), deep * chunk)
            right = w_buf[pl.ds(k * deep, deep), :, cols].reshape(deep * chunk, w_cols)
            acc[...] += jnp.dot(normed[:, lanes], right, preferred_element_type=jnp.float32)
            return 0

        acc[...] = jnp.zeros_like(acc)
        lax.fori_loop(0, count // deep, add, 0)

    def own_block(turn):
        rows = pl.ds(turn * w_cols, w_cols)

        @pl.when(core == 0)
        def _():
            kv_own[rows, :] = acc[...].T.astype(jnp.bfloat16)

        @pl.when(core == 1)
        def _():
            kv_own[rows, :] = acc[...].astype(jnp.bfloat16)

        kv_buf[core, chip, rows, :] = kv_own[rows, :]

    def handed(turn):
        return lambda p, r, q: cross(turn, p, r, q).start()

    def spread(turn):
        first(kv[turn])
        for p in both:
            cross(turn, p, 0, 0).start()

    def arrived(turn):
        for part in both:
            for r in rings:
                for q in rings:
                    rows = kv_rows(part, turn, None)
                    block = kv_buf.at[1 - core, kv[turn][part][3](r, q), rows, :]
                    index = rings[r] * 4 + rings[q]
                    pltpu.make_async_copy(
                        block, block, pair_recv.at[2 * turn + part, index]
                    ).wait()

    finish(w[0])
    project(0)
    own_block(0)
    spread(0)
    first(w[1])
    near(kv[0], handed(0))
    near(w[1])
    relay(kv[0], 0, handed(0))
    far(kv[0], handed(0))
    for r in (-1, 1, 2):
        relay(kv[0], r, handed(0))
    relay(w[1], 0)
    far(w[1])
    relay(w[1], -1)
    finish(kv[0], handed(0))
    arrived(0)
    query_in.wait()

    def sent(turn):
        for part in both:
            for r in rings:
                for q in rings:
                    cross(turn, part, r, q).wait_send()

    width = CHUNK_HEADS * HD
    chunks = q_ref.shape[1] // width
    middle = chunks // 2
    per_kv = 16 // CHUNK_HEADS
    rate = math.log2(math.e) / math.sqrt(HD)

    def hop(c):
        return pltpu.make_async_remote_copy(
            src_ref=stage.at[c], dst_ref=landed.at[c],
            send_sem=hop_send.at[c], recv_sem=hop_recv.at[c],
            device_id={"section": after}, device_id_type=MESH,
        )

    def chain(c):
        cols = pl.ds(pl.multiple_of(c * width, width), width)

        @pl.when(section == 0)
        def _():
            rows = pl.ds(pl.multiple_of(core * tok, tok), tok)
            hidden[...] = jnp.concatenate(
                [joined[2 * c, rows, :], joined[2 * c + 1, rows, :]], axis=1
            )

        @pl.when(section > 0)
        def _():
            hop(c).wait_recv()
            hidden[...] = landed[c]

        fresh = (hidden[...].astype(jnp.float32) + mixed[c]).astype(jnp.bfloat16)
        out_ref[:, cols] = fresh

        @pl.when(section < sections - 1)
        def _():
            stage[c] = fresh
            hop(c).start()

    def attend(i):
        head = i // per_kv
        kcols = pl.ds(pl.multiple_of(head * HD, HD), HD)
        vrows = pl.ds(pl.multiple_of(head // 2 * span, span), span)
        vcols = pl.ds(pl.multiple_of(lax.rem(head, 2) * HD, HD), HD)
        where = [lax.rem(chip + (chips - WINDOW + 1) + b, chips) for b in range(WINDOW)]
        kc = [
            jnp.concatenate([kv_buf[0, b, kcols, :], kx[n]], axis=0) for n, b in enumerate(where)
        ]
        ones = jnp.ones((span, HD), jnp.bfloat16)
        vc = [jnp.concatenate([kv_buf[1, b, vrows, vcols], ones], axis=1) for b in where]
        kc = jnp.concatenate(kc, axis=1)
        vc = jnp.concatenate(vc, axis=0)
        last = (WINDOW - 1) * span
        row = iota((tok, span), 0) + core * tok
        col = iota((tok, span), 1)
        for h in range(CHUNK_HEADS):
            qh = q_ref[:, pl.ds(pl.multiple_of(i * width, width) + h * HD, HD)]
            qc = jnp.concatenate([qh, qx[...]], axis=1)
            s = jnp.dot(qc, kc, preferred_element_type=jnp.float32)
            own = jnp.where(col <= row, s[:, last:], -BIG)
            s = jnp.concatenate([s[:, :last], own], axis=1)
            top = jnp.max(s, axis=1, keepdims=True)
            p = jnp.exp2((s - top) * rate).astype(jnp.bfloat16)
            r = jnp.dot(p, vc, preferred_element_type=jnp.float32)
            mixed[i, :, h * HD : (h + 1) * HD] = r[:, :HD] / r[:, HD:]

    def step(i, _):
        attend(i)
        c = i - section

        @pl.when(((i < middle) & (c >= 0)) | (c >= middle))
        def _():
            chain(c)

        @pl.when(i == 0)
        def _():
            relay(w[1], 1)

        @pl.when(i == 1)
        def _():
            relay(w[1], 2)

        @pl.when(i == 2)
        def _():
            finish(w[1])
            project(1)
            own_block(1)
            spread(1)

        @pl.when(i == 3)
        def _():
            near(kv[1], handed(1))

        @pl.when(i == 4)
        def _():
            relay(kv[1], 0, handed(1))
            far(kv[1], handed(1))

        @pl.when(i == 5)
        def _():
            relay(kv[1], -1, handed(1))
            relay(kv[1], 1, handed(1))

        @pl.when(i == 6)
        def _():
            relay(kv[1], 2, handed(1))

        @pl.when(i == middle - 1)
        def _():
            finish(kv[1], handed(1))

            def catch_up(d, _):
                chain(middle - section + d)
                return 0

            lax.fori_loop(0, section, catch_up, 0)
            arrived(1)

        @pl.when(i == middle)
        def _():
            for gather in (patch, w[0]):
                for _, _, drain, _ in gather:
                    drain()

        @pl.when(i == middle + 1)
        def _():
            for gather in (w[1], kv[0]):
                for _, _, drain, _ in gather:
                    drain()

        @pl.when(i == middle + 2)
        def _():
            sent(0)

        @pl.when(i == middle + 3)
        def _():
            sent(1)

        @pl.when(i == middle + 4)
        def _():
            for _, _, drain, _ in kv[1]:
                drain()

        return 0

    lax.fori_loop(0, chunks, step, 0)

    def tail(d, _):
        chain(chunks - section + d)
        return 0

    lax.fori_loop(0, section, tail, 0)

    @pl.when(section < sections - 1)
    def _():
        def drain(c, _):
            hop(c).wait_send()
            return 0

        lax.fori_loop(0, chunks, drain, 0)

    to_sibling(w_value_ref, w_buf.at[me], 0).wait_send()
    text_pair.wait_send()
    patch_pair.wait_send()
    row_pair.wait_send()


def window(patches, vis_gain, w_merge, counts, offsets, docs, text, gain, w_key, w_value, query):
    count = lax.axis_size("ctx")
    tok, width = text.shape
    chunk = width // count
    kv_width = w_key.shape[1]
    chips = count // 2
    cols = CHUNK_HEADS * HD
    chunks = width // cols
    bf16, f32 = jnp.bfloat16, jnp.float32
    vmem = pl.BlockSpec(memory_space=pltpu.VMEM)
    hbm = pl.BlockSpec(memory_space=pl.ANY)
    dma = pltpu.SemaphoreType.DMA
    return pl.pallas_call(
        window_kernel,
        out_shape=jax.ShapeDtypeStruct((tok, width), bf16),
        in_specs=[vmem, vmem, hbm, vmem, vmem, vmem, hbm, vmem, hbm, hbm, hbm],
        out_specs=vmem,
        scratch_shapes=[
            pltpu.VMEM((2, chips, 16, patches.shape[1] // 2), bf16),
            pltpu.VMEM(w_merge.shape, bf16),
            pltpu.VMEM((count * 8, chunk), bf16),
            pltpu.VMEM((chips, 32, chunk), bf16),
            pltpu.VMEM((2, chips, 32, chunk), bf16),
            pltpu.VMEM((2, tok, width), bf16),
            pltpu.VMEM((count, 2 * tok, chunk), bf16),
            pltpu.VMEM((2 * tok, width), bf16),
            pltpu.VMEM((count, chunk, kv_width), bf16),
            pltpu.VMEM((2 * tok, kv_width // ROUNDS), f32),
            pltpu.VMEM((kv_width, 2 * tok), bf16),
            pltpu.VMEM((2, chips, kv_width, 2 * tok), bf16),
            pltpu.VMEM((tok, width), bf16),
            pltpu.VMEM((2 * tok, 32), bf16),
            pltpu.VMEM((WINDOW, HD, 2 * tok), bf16),
            pltpu.VMEM((tok, HD), bf16),
            pltpu.VMEM((chunks, tok, cols), f32),
            pltpu.VMEM((tok, cols), bf16),
            pltpu.VMEM((chunks, tok, cols), bf16),
            pltpu.VMEM((chunks, tok, cols), bf16),
        ]
        + [dma((2, 20))] * 2
        + [dma((2 * ROUNDS, 20))] * 4
        + [dma((2 * ROUNDS, 16))] * 2
        + [dma((2,)), dma((4,)), dma((4,)), dma((4,)), dma((chunks,)), dma((chunks,))],
        compiler_params=pltpu.CompilerParams(
            collective_id=1, has_side_effects=True, vmem_limit_bytes=60 * 2**20
        ),
        cost_estimate=pl.CostEstimate(
            flops=24 * 10**9, bytes_accessed=12 * 2**20, transcendentals=tok * 64 * 2304
        ),
    )(patches, vis_gain, w_merge, counts, offsets, docs, text, gain, w_key, w_value, query)


def shards(
    text_embeds,
    patches,
    vis_gain,
    w_merge,
    frame_count,
    frame_offset,
    doc_ids,
    norm_gain,
    w_key,
    w_value,
    queries,
):
    count = lax.axis_size("ctx")
    result = window(
        patches,
        vis_gain[None],
        w_merge,
        frame_count[None],
        frame_offset[None],
        doc_ids.reshape(count, 1, -1),
        text_embeds,
        norm_gain,
        w_key[0],
        w_value[0],
        queries[0],
    )
    return result[None]


def solution(mesh):
    return jax.shard_map(
        shards,
        mesh=mesh,
        in_specs=(
            P("ctx", None),
            P("ctx", None),
            P(),
            P(None, "ctx"),
            P(),
            P(),
            P(),
            P("section", None),
            P("section", "ctx", None),
            P("section", "ctx", None),
            P("section", "ctx", None),
        ),
        out_specs=P("section", "ctx", None),
        check_vma=False,
    )
```
